128 devices in a mesh: cells: 16 (over z, y_lo, core), snap: 8 (over y_hi, x).
Axes of the slice: x: 4, y: 4 (y_hi: 2, y_lo: 2; y = y_hi * 2 + y_lo), z: 4, core: 2. Of those that a mesh axis runs over, the one named last changes fastest.
Arguments:
- snapshots: bfloat16 [4096, 65536], P('snap', 'cells'), may hold values from -8 to 8
- pod_basis: bfloat16 [96, 65536], P(None, 'cells'), may hold values from -0.0234375 to 0.0234375
- reference_field: bfloat16 [65536], P('cells'), may hold values from -6 to 6
- ridge_weights: float32 [4752], replicated, may hold values from 0.2 to 2
Outputs:
- trailing_gram: float32 [4752, 4752], P('cells', 'snap')
- panel_factor: float32 [4752, 512], P('cells')
The draws below stay inside these ranges and needn't reach their ends.
All inputs are finite; a program needn't handle non-finite values.
Results may differ from the reference program's by a relative error of at most 0.0003.
Values sent between devices are 32-bit elements; how exact they have to be, the bound alone decides.
No kernel may reach another device: no remote copies, remote signals or barrier semaphores. Data moves between devices by JAX's collectives and lax.ppermute only.
A program may use at most 128 MiB of HBM per device.

```python
import math
import jax
import jax.numpy as jnp
import numpy as np
from jax import lax

R = 96
K = 4752
PANEL = 512
SNAPS = 4096
CELLS = 65536


def draw_snapshots(key, part):
    key = jax.random.fold_in(key, 11)
    key_noise, key_mode, key_amplitude = jax.random.split(key, 3)
    noise_part = jax.random.normal(key_noise, (SNAPS, CELLS), jnp.float32)
    row_scale = jnp.ones((SNAPS, 1), jnp.float32)
    amplitude = 1.0 + 0.5 * jax.random.normal(key_amplitude, (SNAPS, 1), jnp.float32)
    cell_mode = jax.random.normal(key_mode, (1, CELLS), jnp.float32)
    snapshot = 0.6 * row_scale * noise_part + 0.6 * amplitude * cell_mode
    return jnp.clip(snapshot, -8.0, 8.0).astype(jnp.bfloat16)


def steps_of(stream_key, shape, cuts, least, high):
    def one(position, shards_of):
        steps = jax.random.uniform(jax.random.fold_in(jax.random.fold_in(stream_key, 6), position), (shards_of,), jnp.float32, least / len(cuts), high / len(cuts))
        return jnp.repeat(jnp.exp(steps), shape[position] // shards_of).reshape((-1,) + (1,) * (len(shape) - position - 1))

    factor_of = one(*cuts[0])
    for cut in cuts[1:]:
        factor_of = factor_of * one(*cut)
    return factor_of


def gaussian(own_key, extent, spread, limit, cuts=(), held_as=jnp.bfloat16):
    factor_of = steps_of(own_key, extent, cuts, -0.22, 0.18) if cuts else 1.0
    result = jax.random.normal(own_key, extent, jnp.float32) * spread * factor_of
    return jnp.minimum(jnp.maximum(result, -limit), limit).astype(held_as)


def setup_inputs(seed: int = 0) -> dict:
    streams_of = jax.random.split(jax.random.key(seed), 5)
    return {
        "snapshots": draw_snapshots(jax.random.fold_in(streams_of[4], 71), 0),
        "pod_basis": gaussian(streams_of[1], (R, CELLS), CELLS ** -0.5, 0.0234375, ((1, 16),)),
        "reference_field": gaussian(streams_of[2], (CELLS,), 1.0, 6.0, ((0, 16),)),
        "ridge_weights": jnp.clip(jnp.exp(jax.random.uniform(streams_of[3], (K,), jnp.float32, math.log(0.2), math.log(2.0))), 0.2, 2.0),
    }


def feature_matrix(coeffs):
    column_count = coeffs.shape[1]
    upper_rows, upper_cols = np.triu_indices(column_count)
    quadratic = coeffs[:, upper_rows] * coeffs[:, upper_cols]
    return jnp.concatenate([coeffs, quadratic], axis=1)

def reference(snapshots, pod_basis, reference_field, ridge_weights):
    projected = jnp.dot(snapshots.astype(jnp.float32), pod_basis.T.astype(jnp.float32), preferred_element_type=jnp.float32)
    offset = jnp.dot(reference_field[None, :].astype(jnp.float32), pod_basis.T.astype(jnp.float32), preferred_element_type=jnp.float32)
    coeffs = projected - offset
    features = feature_matrix(coeffs)
    snap_total = features.shape[0]
    gram_matrix = jnp.dot(features.T, features, precision=lax.Precision.HIGHEST) / snap_total
    gram_matrix = gram_matrix + jnp.diag(ridge_weights)
    corner_factor = jnp.linalg.cholesky(gram_matrix[:PANEL, :PANEL])
    lower_part = lax.linalg.triangular_solve(corner_factor, gram_matrix[PANEL:, :PANEL], left_side=False, lower=True, transpose_a=True)
    panel_factor = jnp.concatenate([corner_factor, lower_part], axis=0)
    update = jnp.dot(lower_part, lower_part.T, precision=lax.Precision.HIGHEST)
    trailing_gram = gram_matrix.at[PANEL:, PANEL:].add(-update)
    return (trailing_gram, panel_factor)
```

```python
import jax
import jax.numpy as jnp
import numpy as np
from jax import lax
from jax.sharding import PartitionSpec as P

PANEL = 512


def feature_pairs(column_count):
    upper_rows, upper_cols = np.triu_indices(column_count)
    left_table = np.concatenate([np.arange(column_count), upper_rows]).astype(np.int32)
    right_table = np.concatenate([np.full(column_count, column_count), upper_cols]).astype(np.int32)
    return (left_table, right_table)


def feature_block(coeffs, first_col, column_count):
    modes = coeffs.shape[0]
    left_table, right_table = feature_pairs(modes)
    left_index = lax.dynamic_slice_in_dim(jnp.asarray(left_table), first_col, column_count)
    right_index = lax.dynamic_slice_in_dim(jnp.asarray(right_table), first_col, column_count)
    extended = jnp.concatenate([coeffs, jnp.ones((1, coeffs.shape[1]), jnp.float32)], axis=0)
    slot = jnp.arange(modes + 1, dtype=jnp.int32)[None, :]
    left_pick = (slot == left_index[:, None]).astype(jnp.float32)
    right_pick = (slot == right_index[:, None]).astype(jnp.float32)
    left_values = jnp.dot(left_pick, extended, precision=lax.Precision.HIGHEST)
    right_values = jnp.dot(right_pick, extended, precision=lax.Precision.HIGHEST)
    return left_values * right_values


def gram_block(left_features, right_features, snap_total):
    product = lax.dot_general(
        left_features,
        right_features,
        (((1,), (1,)), ((), ())),
        precision=lax.Precision.HIGH,
        preferred_element_type=jnp.float32,
    )
    return product / snap_total


def add_ridge(gram_part, ridge_weights, first_row, first_col):
    rows_global = first_row + jnp.arange(gram_part.shape[0], dtype=jnp.int32)
    cols_global = first_col + jnp.arange(gram_part.shape[1], dtype=jnp.int32)
    ridge_rows = lax.dynamic_slice_in_dim(ridge_weights, first_row, gram_part.shape[0])
    return gram_part + jnp.where(
        rows_global[:, None] == cols_global[None, :], ridge_rows[:, None], 0.0
    )


def panel_block(features, first_row, panel_features, corner_factor, corner_inverse, ridge_weights, snap_total):
    block_rows = features.shape[0]
    panel_width = corner_factor.shape[0]
    gram_part = add_ridge(
        gram_block(features, panel_features, snap_total), ridge_weights, first_row, 0
    )
    solved = lax.dot_general(
        gram_part, corner_inverse, (((1,), (1,)), ((), ())),
        precision=lax.Precision.HIGHEST, preferred_element_type=jnp.float32,
    )
    padded = jnp.concatenate(
        [corner_factor, jnp.zeros((block_rows, panel_width), jnp.float32)], axis=0
    )
    factor_rows = lax.dynamic_slice_in_dim(
        padded, jnp.minimum(first_row, panel_width), block_rows, 0
    )
    inside = first_row + jnp.arange(block_rows, dtype=jnp.int32) < panel_width
    return jnp.where(inside[:, None], factor_rows, solved)


def swap(value, axis, bit):
    size = lax.axis_size(axis)
    return lax.ppermute(value, axis, [(i, i ^ bit) for i in range(size)])


def all_coeffs(partial):
    modes, snaps = partial.shape
    half = snaps // 2
    core = lax.axis_index("cells") & 1
    group = lax.axis_index("snap")
    keep = lax.dynamic_slice_in_dim(partial, core * half, half, 1)
    send = lax.dynamic_slice_in_dim(partial, (1 - core) * half, half, 1)
    total = keep + swap(send, "cells", 1)
    for bit in (2, 4, 8):
        total = total + swap(total, "cells", bit)
    blocks = total[None]
    for bit in (4, 2, 1):
        blocks = jnp.concatenate([blocks, swap(blocks, "snap", bit)], axis=0)
    both = jnp.stack([blocks, swap(blocks, "cells", 1)])
    ordered = []
    for g in range(8):
        x = group ^ g
        place = ((x >> 2) & 1) + (x & 2) + ((x & 1) << 2)
        for c in range(2):
            ordered.append(both[core ^ c, place])
    return jnp.concatenate(ordered, axis=1)


def per_device(snapshots, pod_basis, reference_field, ridge_weights):
    contract = (((1,), (1,)), ((), ()))
    projected = lax.dot_general(pod_basis, snapshots, contract, preferred_element_type=jnp.float32)
    offset = lax.dot_general(
        pod_basis, reference_field[None, :], contract, preferred_element_type=jnp.float32
    )
    coeffs = all_coeffs(projected - offset)
    snap_total = coeffs.shape[1]
    feature_total = ridge_weights.shape[0]
    row_count = feature_total // lax.axis_size("cells")
    col_count = feature_total // lax.axis_size("snap")
    first_row = lax.axis_index("cells") * row_count
    first_col = lax.axis_index("snap") * col_count
    panel_features = feature_block(coeffs, 0, PANEL)
    row_features = feature_block(coeffs, first_row, row_count)
    col_features = feature_block(coeffs, first_col, col_count)
    corner = add_ridge(gram_block(panel_features, panel_features, snap_total), ridge_weights, 0, 0)
    corner_factor = jnp.linalg.cholesky(corner)
    corner_inverse = lax.linalg.triangular_solve(
        corner_factor, jnp.eye(PANEL, dtype=jnp.float32), left_side=True, lower=True
    )
    own_rows = panel_block(
        row_features, first_row, panel_features, corner_factor, corner_inverse, ridge_weights, snap_total
    )
    col_rows = panel_block(
        col_features, first_col, panel_features, corner_factor, corner_inverse, ridge_weights, snap_total
    )
    tile = add_ridge(
        gram_block(row_features, col_features, snap_total), ridge_weights, first_row, first_col
    )
    update = lax.dot_general(
        own_rows,
        col_rows,
        contract,
        precision=lax.Precision.HIGHEST,
        preferred_element_type=jnp.float32,
    )
    rows_global = first_row + jnp.arange(row_count, dtype=jnp.int32)
    cols_global = first_col + jnp.arange(col_count, dtype=jnp.int32)
    trailing = (rows_global[:, None] >= PANEL) & (cols_global[None, :] >= PANEL)
    trailing_gram = jnp.where(trailing, tile - update, tile)
    return (trailing_gram, own_rows)


def solution(mesh):
    return jax.shard_map(
        per_device,
        mesh=mesh,
        in_specs=(P("snap", "cells"), P(None, "cells"), P("cells"), P()),
        out_specs=(P("cells", "snap"), P("cells", None)),
        check_vma=False,
    )
```

```python
import functools
import jax
import jax.numpy as jnp
import numpy as np
from jax import lax
from jax.experimental import pallas as pl
from jax.experimental.pallas import tpu as pltpu
from jax.sharding import PartitionSpec as P

PANEL = 512
HALF = 256
BLOCK = 128
STEP = 32
CHUNKS = 16
SLOTS = 112
HI = lax.Precision.HIGHEST
F32 = jnp.float32
BF16 = jnp.bfloat16
NT = (((1,), (1,)), ((), ()))
TN = (((0,), (0,)), ((), ()))
NN = (((1,), (0,)), ((), ()))


def dot(a, b, dims, precision=None):
    return lax.dot_general(a, b, dims, precision=precision, preferred_element_type=F32)


def split(value):
    high = value.astype(BF16)
    return high, (value - high.astype(F32)).astype(BF16)


def dot3(a, b):
    ah, al = a
    bh, bl = b
    return dot(jnp.concatenate([ah, ah, al], 1), jnp.concatenate([bh, bl, bh], 1), NT)


def pick_tables(first, rows, modes):
    index = first + lax.broadcasted_iota(jnp.int32, (rows, 128), 0)
    slot = lax.broadcasted_iota(jnp.int32, (rows, 128), 1)

    def offset(a):
        return modes + modes * a - (a * (a - 1)) // 2

    linear = index < modes
    here = (index >= offset(slot)) & (index < offset(slot + 1)) & (slot < modes)
    right_value = jnp.where(here, index - offset(slot) + slot, 0).astype(F32)
    right_index = jnp.sum(right_value, axis=1, keepdims=True).astype(jnp.int32)
    left_index = jnp.sum(jnp.where(here, slot, 0).astype(F32), axis=1, keepdims=True).astype(jnp.int32)
    left_index = jnp.where(linear, index, left_index)
    right_index = jnp.where(linear, modes, right_index)
    return (slot == left_index).astype(F32), (slot == right_index).astype(F32)


def pick_kernel(modes, scal, lr, rr, lc, rc):
    for ref_l, ref_r, first in ((lr, rr, scal[0]), (lc, rc, scal[1])):
        rows = ref_l.shape[0]
        left, right = pick_tables(first, rows, modes)
        for ref, value in ((ref_l, left), (ref_r, right)):
            ref[:, 0:SLOTS] = value[:, 0:SLOTS].astype(BF16)
            ref[:, SLOTS : 2 * SLOTS] = value[:, 0:SLOTS].astype(BF16)


def picks(scal, row_pad, col_pad, modes):
    shapes = [(row_pad, 2 * SLOTS)] * 2 + [(col_pad, 2 * SLOTS)] * 2
    return pl.pallas_call(
        functools.partial(pick_kernel, modes),
        in_specs=[pl.BlockSpec(memory_space=pltpu.SMEM)],
        out_shape=[jax.ShapeDtypeStruct(s, BF16) for s in shapes],
        compiler_params=pltpu.CompilerParams(vmem_limit_bytes=40 * 2**20),
        name="picks",
    )(scal)


def panel_features(c_ref, t, f_ref, modes):
    f_ref[0:modes, :] = c_ref[t]
    at, a = modes, 0
    while at < PANEL:
        count = min(modes - a, PANEL - at)
        f_ref[at : at + count, :] = c_ref[t, a : a + count, :] * c_ref[t, a : a + 1, :]
        at += count
        a += 1


def corner_chunk(t, scal, own, oth, c_s, f_s, fh, fl, a_s, modes):
    g, side = t // 2, t % 2
    place = g ^ scal[2]
    place = ((place >> 2) & 1) + (place & 2) + ((place & 1) << 2)
    mine = side == scal[3]
    c_s[t] = jnp.where(mine, own[place], oth[place])
    panel_features(c_s, t, f_s, modes)
    h, l = split(f_s[...])
    fh[t] = h
    fl[t] = l
    a_s[0:HALF, :] += dot3((h[0:HALF], l[0:HALF]), (h, l))
    a_s[HALF:, HALF:] += dot3((h[HALF:], l[HALF:]), (h[HALF:], l[HALF:]))


def lane_bcast(x, c):
    return jnp.broadcast_to(x[:, c : c + 1], (8, 128))


def sub_bcast(x, k):
    return jnp.broadcast_to(x[k : k + 1, :], (8, 128))


def factor_micro(T, b, q):
    sub = lax.broadcasted_iota(jnp.int32, (8, 128), 0)
    B = {(r, k): lane_bcast(T[r][0], STEP * b + 8 * q + k) for r in range(q, 4) for k in range(8)}
    scale = None
    for k in range(8):
        rs = lax.rsqrt(sub_bcast(B[q, k], k))
        inv = rs * rs
        scale = rs if scale is None else jnp.where(sub == k, rs, scale)
        row = [sub_bcast(part, k) for part in T[q]]
        pivots = {j: sub_bcast(B[q, j], k) for j in range(k + 1, 8)}
        for r in range(q, 4):
            m = B[r, k] * inv
            if r == q:
                m = jnp.where(sub > k, m, 0.0)
            for j in range(k + 1, 8):
                B[r, j] = B[r, j] - m * pivots[j]
            T[r] = [part - m * line for part, line in zip(T[r], row)]
    T[q] = [part * scale for part in T[q]]


def factor_step(s_ref, b, between):
    lo = STEP * b
    T = [[s_ref[lo + 8 * r : lo + 8 * r + 8, 0:128], s_ref[lo + 8 * r : lo + 8 * r + 8, 128:256]] for r in range(4)]
    for q in range(4):
        factor_micro(T, b, q)
        between(4 * b + q)
    for r in range(4):
        s_ref[lo + 8 * r : lo + 8 * r + 8, 0:128] = T[r][0]
        s_ref[lo + 8 * r : lo + 8 * r + 8, 128:256] = T[r][1]
    if b < 3:
        full = s_ref[lo : lo + STEP, :]
        upd = dot(s_ref[lo : lo + STEP, 0:128], full, TN, HI)
        s_ref[lo + STEP : 128, :] -= upd[lo + STEP :, :]


def factor_block(k, a_s, s_ref, u_s, inv_s, between):
    ri = lax.broadcasted_iota(jnp.int32, (BLOCK, BLOCK), 0)
    ci = lax.broadcasted_iota(jnp.int32, (BLOCK, BLOCK), 1)
    s_ref[:, 0:BLOCK] = a_s[0:BLOCK, 0:BLOCK]
    s_ref[:, BLOCK:] = (ri == ci).astype(F32)
    for b in range(4):
        factor_step(s_ref, b, between)
    inverse = s_ref[:, BLOCK:]
    inv_s[k] = inverse
    rest = dot(inverse, a_s[0:BLOCK, BLOCK:], NN, HI)
    u_s[k, :, 0:BLOCK] = jnp.where(ci >= ri, s_ref[:, 0:BLOCK], 0.0)
    u_s[k, :, BLOCK:] = rest
    left = a_s[BLOCK:, BLOCK:] - dot(rest, rest, TN, HI)
    a_s[0 : PANEL - BLOCK, 0 : PANEL - BLOCK] = left


def stacked(c, modes):
    n = c.shape[1]
    high, low = split(c)
    gap = lax.broadcasted_iota(jnp.int32, (SLOTS - modes, n), 0)
    ones = (gap == 0).astype(F32).astype(BF16)
    none = jnp.zeros((SLOTS - modes, n), BF16)
    return jnp.concatenate([high, ones, low, none], axis=0)


def picked(left, right, cs):
    return split(dot(left, cs, NN) * dot(right, cs, NN))


def block_parts(t, c_s, fh, fl, lr, rr, lc, rc, gr, gc, gt, modes):
    env = {}

    def part0():
        cs = stacked(c_s[t], modes)
        env["fr"] = picked(lr[...], rr[...], cs)
        env["fc"] = picked(lc[...], rc[...], cs)
        env["fp"] = (fh[t], fl[t])

    def part1():
        gr[...] += dot3(env["fr"], env["fp"])

    def part2():
        gc[...] += dot3(env["fc"], env["fp"])

    def part3():
        gt[...] += dot3(env["fr"], env["fc"])

    return [part0, part1, part2, part3]


def solve_rows(g, u_s, inv_s, p_ref):
    for k in range(4):
        lo = BLOCK * k
        value = g[:, lo : lo + BLOCK]
        for j in range(k):
            off = lo - BLOCK * j
            value = value - dot(p_ref[:, BLOCK * j : BLOCK * j + BLOCK], u_s[j, :, off : off + BLOCK], NN, HI)
        p_ref[:, lo : lo + BLOCK] = dot(value, inv_s[k], NT, HI)


def main_kernel(modes, snap_total, scal, own, oth, lr, rr, lc, rc, ridge_panel, ridge_cols,
                tile_out, rows_out,
                c_s, f_s, fh, fl, a_s, s_s, u_s, inv_s, gr, gc, gt, pr, pc):
    a_s[...] = jnp.zeros_like(a_s)
    gr[...] = jnp.zeros_like(gr)
    gc[...] = jnp.zeros_like(gc)
    gt[...] = jnp.zeros_like(gt)

    def corner_body(t, carry):
        corner_chunk(t, scal, own, oth, c_s, f_s, fh, fl, a_s, modes)
        return carry

    lax.fori_loop(0, CHUNKS, corner_body, 0)
    ri = lax.broadcasted_iota(jnp.int32, (PANEL, PANEL), 0)
    ci = lax.broadcasted_iota(jnp.int32, (PANEL, PANEL), 1)
    a_s[...] = a_s[...] * (1.0 / snap_total) + jnp.where(ri == ci, ridge_panel[...], 0.0)

    def parts_of(t):
        return block_parts(t, c_s, fh, fl, lr, rr, lc, rc, gr, gc, gt, modes)

    def block_body(k, carry):
        parts = []
        for b in range(4):
            parts += parts_of(4 * k + b)
        factor_block(k, a_s, s_s, u_s, inv_s, lambda i: parts[i]())
        return carry

    lax.fori_loop(0, 4, block_body, 0)

    first_row, first_col = scal[0], scal[1]
    inv_total = 1.0 / snap_total
    for g, p, first in ((gr, pr, first_row), (gc, pc, first_col)):
        rows = g.shape[0]
        ri = first + lax.broadcasted_iota(jnp.int32, (rows, PANEL), 0)
        ci = lax.broadcasted_iota(jnp.int32, (rows, PANEL), 1)
        g[...] = g[...] * inv_total + jnp.where(ri == ci, ridge_panel[...], 0.0)
        solve_rows(g, u_s, inv_s, p)

    rows, cols = tile_out.shape
    total = gt[...] * inv_total
    ri = first_row + lax.broadcasted_iota(jnp.int32, total.shape, 0)
    ci = first_col + lax.broadcasted_iota(jnp.int32, total.shape, 1)
    total = total + jnp.where(ri == ci, ridge_cols[...], 0.0)
    update = dot3(split(pr[...]), split(pc[...]))
    total = jnp.where((ri >= PANEL) & (ci >= PANEL), total - update, total)
    tile_out[...] = total[0:rows, 0:cols]
    line = first_row + lax.broadcasted_iota(jnp.int32, (rows, PANEL), 0)
    at = lax.broadcasted_iota(jnp.int32, (rows, PANEL), 1)
    rows_out[...] = jnp.where(at <= line, pr[0:rows, :], 0.0)


def main(scal, own, oth, tables, ridge_panel, ridge_cols, rows, cols, snap_total):
    modes = own.shape[1]
    n = own.shape[2]
    lr, rr, lc, rc = tables
    row_pad, col_pad = lr.shape[0], lc.shape[0]
    vmem = pl.BlockSpec(memory_space=pltpu.VMEM)
    return pl.pallas_call(
        functools.partial(main_kernel, modes, snap_total),
        in_specs=[pl.BlockSpec(memory_space=pltpu.SMEM)] + [vmem] * 8,
        out_specs=[vmem, vmem],
        out_shape=[jax.ShapeDtypeStruct((rows, cols), F32), jax.ShapeDtypeStruct((rows, PANEL), F32)],
        scratch_shapes=[
            pltpu.VMEM((CHUNKS, modes, n), F32),
            pltpu.VMEM((PANEL, n), F32),
            pltpu.VMEM((CHUNKS, PANEL, n), BF16),
            pltpu.VMEM((CHUNKS, PANEL, n), BF16),
            pltpu.VMEM((PANEL, PANEL), F32),
            pltpu.VMEM((BLOCK, 2 * BLOCK), F32),
            pltpu.VMEM((4, BLOCK, PANEL), F32),
            pltpu.VMEM((4, BLOCK, BLOCK), F32),
            pltpu.VMEM((row_pad, PANEL), F32),
            pltpu.VMEM((col_pad, PANEL), F32),
            pltpu.VMEM((row_pad, col_pad), F32),
            pltpu.VMEM((row_pad, PANEL), F32),
            pltpu.VMEM((col_pad, PANEL), F32),
        ],
        compiler_params=pltpu.CompilerParams(vmem_limit_bytes=60 * 2**20),
        name="gram_factor",
    )(scal, own, oth, lr, rr, lc, rc, ridge_panel, ridge_cols)


def swap(value, axis, bit):
    size = lax.axis_size(axis)
    return lax.ppermute(value, axis, [(i, i ^ bit) for i in range(size)])


def gather_coeffs(partial, core):
    half = partial.shape[1] // 2
    keep = lax.dynamic_slice_in_dim(partial, core * half, half, 1)
    send = lax.dynamic_slice_in_dim(partial, (1 - core) * half, half, 1)
    total = keep + swap(send, "cells", 1)
    for bit in (2, 4, 8):
        total = total + swap(total, "cells", bit)
    blocks = total[None]
    for bit in (4, 2, 1):
        blocks = jnp.concatenate([blocks, swap(blocks, "snap", bit)], axis=0)
    return blocks, swap(blocks, "cells", 1)


def padded(count):
    return -(-count // 16) * 16


def per_device(snapshots, pod_basis, reference_field, ridge_weights):
    contract = (((1,), (1,)), ((), ()))
    modes = pod_basis.shape[0]
    snap_total = snapshots.shape[0] * lax.axis_size("snap")
    feature_total = ridge_weights.shape[0]
    rows = feature_total // lax.axis_size("cells")
    cols = feature_total // lax.axis_size("snap")
    group = lax.axis_index("snap")
    core = lax.axis_index("cells") & 1
    first_row = lax.axis_index("cells") * rows
    first_col = group * cols
    scal = jnp.stack([first_row, first_col, group, core]).astype(jnp.int32)
    tables = picks(scal, padded(rows), padded(cols), modes)
    ridge_panel = ridge_weights[None, :PANEL]
    ridge_cols = lax.dynamic_slice_in_dim(ridge_weights, first_col, cols)
    ridge_cols = jnp.pad(ridge_cols, (0, padded(cols) - cols))[None, :]

    projected = lax.dot_general(pod_basis, snapshots, contract, preferred_element_type=F32)
    offset = lax.dot_general(pod_basis, reference_field[None, :], contract, preferred_element_type=F32)
    own, other = gather_coeffs(projected - offset, core)
    return tuple(main(scal, own, other, tables, ridge_panel, ridge_cols, rows, cols, snap_total))


def solution(mesh):
    return jax.shard_map(
        per_device,
        mesh=mesh,
        in_specs=(P("snap", "cells"), P(None, "cells"), P("cells"), P()),
        out_specs=(P("cells", "snap"), P("cells", None)),
        check_vma=False,
    )
```

```python
import functools
import jax
import jax.numpy as jnp
import numpy as np
from jax import lax
from jax.experimental import pallas as pl
from jax.experimental.pallas import tpu as pltpu
from jax.sharding import PartitionSpec as P

PANEL = 512
HALF = 256
BLOCK = 128
STEP = 32
SLOTS = 112
F32 = jnp.float32
BF16 = jnp.bfloat16
NT = (((1,), (1,)), ((), ()))
TN = (((0,), (0,)), ((), ()))
NN = (((1,), (0,)), ((), ()))


def dot(a, b, dims, precision=None):
    return lax.dot_general(a, b, dims, precision=precision, preferred_element_type=F32)


def split(value):
    high = value.astype(BF16)
    return high, (value - high.astype(F32)).astype(BF16)


def dot3(a, b):
    ah, al = a
    bh, bl = b
    return dot(jnp.concatenate([ah, ah, al], 1), jnp.concatenate([bh, bl, bh], 1), NT)


def pick_tables(first, rows, modes):
    index = first + lax.broadcasted_iota(jnp.int32, (rows, 128), 0)
    slot = lax.broadcasted_iota(jnp.int32, (rows, 128), 1)

    def offset(a):
        return modes + modes * a - (a * (a - 1)) // 2

    linear = index < modes
    here = (index >= offset(slot)) & (index < offset(slot + 1)) & (slot < modes)
    right_value = jnp.where(here, index - offset(slot) + slot, 0).astype(F32)
    right_index = jnp.sum(right_value, axis=1, keepdims=True).astype(jnp.int32)
    left_index = jnp.sum(jnp.where(here, slot, 0).astype(F32), axis=1, keepdims=True).astype(jnp.int32)
    left_index = jnp.where(linear, index, left_index)
    right_index = jnp.where(linear, modes, right_index)
    return (slot == left_index).astype(F32), (slot == right_index).astype(F32)


def pick_kernel(modes, scale, scal, lr, rr, lc, rc):
    for ref_l, ref_r, first in ((lr, rr, scal[0]), (lc, rc, scal[1])):
        rows = ref_l.shape[0]
        left, right = pick_tables(first, rows, modes)
        left = left * scale
        for ref, value in ((ref_l, left), (ref_r, right)):
            ref[:, 0:SLOTS] = value[:, 0:SLOTS].astype(BF16)
            ref[:, SLOTS : 2 * SLOTS] = value[:, 0:SLOTS].astype(BF16)


def picks(scal, row_pad, col_pad, modes, scale):
    shapes = [(row_pad, 2 * SLOTS)] * 2 + [(col_pad, 2 * SLOTS)] * 2
    return pl.pallas_call(
        functools.partial(pick_kernel, modes, scale),
        in_specs=[pl.BlockSpec(memory_space=pltpu.SMEM)],
        out_shape=[jax.ShapeDtypeStruct(s, BF16) for s in shapes],
        compiler_params=pltpu.CompilerParams(vmem_limit_bytes=40 * 2**20),
        name="picks",
    )(scal)


def panel_features(c_ref, t, f_ref, modes, scale):
    f_ref[0:modes, :] = c_ref[t] * scale
    at, a = modes, 0
    while at < PANEL:
        count = min(modes - a, PANEL - at)
        f_ref[at : at + count, :] = c_ref[t, a : a + count, :] * (c_ref[t, a : a + 1, :] * scale)
        at += count
        a += 1


def panel_pair(t, c_s, f_s, fh, fl, modes, scale):
    for i in range(2):
        panel_features(c_s, t + i, f_s.at[i], modes, scale)
        fh[t + i], fl[t + i] = split(f_s[i])


def corner_pair(t, fh, fl, a_ref):
    pairs = [(fh[t + i], fl[t + i]) for i in range(2)]
    top = [dot3((h[0:HALF], l[0:HALF]), (h, l)) for h, l in pairs]
    low = [dot3((h[HALF:], l[HALF:]), (h[HALF:], l[HALF:])) for h, l in pairs]
    a_ref[0:HALF, :] = top[0] + top[1]
    a_ref[HALF:, HALF:] = low[0] + low[1]


def lane_bcast(x, c):
    return jnp.broadcast_to(x[:, c : c + 1], (8, 128))


def sub_bcast(x, k):
    return jnp.broadcast_to(x[k : k + 1, :], (8, 128))


def split3(value):
    high = value.astype(BF16)
    rest = value - high.astype(F32)
    middle = rest.astype(BF16)
    return high, middle, (rest - middle.astype(F32)).astype(BF16)


def update_dot(left, right):
    lh, lm, ll = split3(left)
    rh, rm, rl = split3(right)
    return dot(
        jnp.concatenate([lh, lh, lh, lm, lm, ll], 0), jnp.concatenate([rh, rm, rl, rh, rm, rh], 0), TN
    )


def dot_split(a, b, dims):
    ah, al = a
    bh, bl = b
    return dot(ah, bh, dims) + (dot(ah, bl, dims) + dot(al, bh, dims))


def factor_step(s_ref, b, between):
    lo = STEP * b
    strips = STEP // 8
    sub = lax.broadcasted_iota(jnp.int32, (8, 128), 0)
    T = [[s_ref[lo + 8 * r : lo + 8 * r + 8, 0:128], s_ref[lo + 8 * r : lo + 8 * r + 8, 128:256]] for r in range(strips)]
    B = {(r, j): lane_bcast(T[r][0], lo + j) for j in range(STEP) for r in range(j // 8, strips)}
    for q in range(strips):
        scale = None
        for k in range(8 * q, 8 * q + 8):
            rs = lax.rsqrt(sub_bcast(B[q, k], k - 8 * q))
            inv = rs * rs
            scale = rs if scale is None else jnp.where(sub == k - 8 * q, rs, scale)
            row = [sub_bcast(part, k - 8 * q) for part in T[q]]
            pivots = {j: sub_bcast(B[j // 8, k], j % 8) for j in range(k + 1, STEP)}
            for r in range(q, strips):
                m = B[r, k] * inv
                if r == q:
                    m = jnp.where(sub > k - 8 * q, m, 0.0)
                for j in range(k + 1, STEP):
                    if j // 8 <= r:
                        B[r, j] = B[r, j] - m * pivots[j]
                T[r] = [part - m * line for part, line in zip(T[r], row)]
        T[q] = [part * scale for part in T[q]]
        between(4 * b + q)
    for r in range(strips):
        s_ref[lo + 8 * r : lo + 8 * r + 8, 0:128] = T[r][0]
        s_ref[lo + 8 * r : lo + 8 * r + 8, 128:256] = T[r][1]
    if b < 3:
        full = s_ref[lo : lo + STEP, :]
        upd = update_dot(full[:, 0:128], full)
        s_ref[lo + STEP : 128, :] -= upd[lo + STEP :, :]


def factor_block(k, a_s, s_ref, e_s, u_s, inv_s, low_s, between):
    ri = lax.broadcasted_iota(jnp.int32, (BLOCK, BLOCK), 0)
    ci = lax.broadcasted_iota(jnp.int32, (BLOCK, BLOCK), 1)
    s_ref[:, 0:BLOCK] = a_s[0:BLOCK, 0:BLOCK]
    s_ref[:, BLOCK:] = (ri == ci).astype(F32)
    for b in range(4):
        factor_step(s_ref, b, between)
    inverse = s_ref[:, BLOCK:]
    inv_s[k] = inverse
    inv_parts = split(inverse)
    rest = dot_split(inv_parts, split(a_s[0:BLOCK, BLOCK:]), NN)
    parts = split(rest)
    a_s[0 : PANEL - BLOCK, 0 : PANEL - BLOCK] = a_s[BLOCK:, BLOCK:] - dot_split(parts, parts, TN)
    u_s[k, :, 0:BLOCK] = jnp.where(ci >= ri, s_ref[:, 0:BLOCK], 0.0)
    u_s[k, :, BLOCK:] = rest
    low_s[k] = dot_split(inv_parts, split(e_s[...]), NN)
    e_s[...] = -dot_split((parts[0][:, 0:BLOCK], parts[1][:, 0:BLOCK]), inv_parts, TN)


def stacked(c, modes):
    n = c.shape[1]
    high, low = split(c)
    gap = lax.broadcasted_iota(jnp.int32, (SLOTS - modes, n), 0)
    ones = (gap == 0).astype(F32).astype(BF16)
    none = jnp.zeros((SLOTS - modes, n), BF16)
    return jnp.concatenate([high, ones, low, none], axis=0)


def picked(left, right, cs):
    return split(dot(left, cs, NN) * dot(right, cs, NN))


def block_parts(t, c_s, fh, fl, lr, rr, lc, rc, gr, gc, gt, modes):
    env = {}

    def part0():
        cs = stacked(c_s[t], modes)
        env["fr"] = picked(lr[...], rr[...], cs)
        env["fc"] = picked(lc[...], rc[...], cs)
        env["fp"] = (fh[t], fl[t])

    def part1():
        gr[...] += dot3(env["fr"], env["fp"])

    def part2():
        gc[...] += dot3(env["fc"], env["fp"])

    def part3():
        gt[...] += dot3(env["fr"], env["fc"])

    return [part0, part1, part2, part3]


def pair_inverse(p, inv_s, low_s):
    zero = jnp.zeros((BLOCK, BLOCK), F32)
    top = jnp.concatenate([inv_s[2 * p], zero], 1)
    return split(jnp.concatenate([top, jnp.concatenate([low_s[2 * p + 1], inv_s[2 * p + 1]], 1)], 0))


def solve_rows(g, inverses, cross, p_ref):
    first = dot_split(split(g[:, 0:HALF]), inverses[0], NT)
    p_ref[:, 0:HALF] = first
    value = g[:, HALF:] - dot_split(split(first), cross, NN)
    p_ref[:, HALF:] = dot_split(split(value), inverses[1], NT)


def diagonal(shape, first_row, first_col, values):
    ri = first_row + lax.broadcasted_iota(jnp.int32, shape, 0)
    ci = first_col + lax.broadcasted_iota(jnp.int32, shape, 1)
    return jnp.where(ri == ci, values, 0.0)


def diagonal(shape, first_row, first_col, values):
    ri = first_row + lax.broadcasted_iota(jnp.int32, shape, 0)
    ci = first_col + lax.broadcasted_iota(jnp.int32, shape, 1)
    return jnp.where(ri == ci, values, 0.0)


def early_kernel(modes, scale, first, extra, *refs):
    own, oth, lr, rr, lc, rc = refs[0:6]
    if first:
        scal, ridge_panel, ridge_cols = refs[6:9]
        a_out, gr, gc, gt, c_s, f_s, fh, fl, a_s = refs[9:]
        gr[...] = jnp.zeros_like(gr)
        gc[...] = diagonal(gc.shape, scal[1], 0, ridge_panel[...])
        gt[...] = diagonal(gt.shape, scal[0], scal[1], ridge_cols[...])
    else:
        gr_in, gc_in, gt_in = refs[6:9]
        a_out, gr, gc, gt, c_s, f_s, fh, fl, a_s, pair_s = refs[9:]
        gc[...] = gc_in[...]
        gt[...] = gt_in[...]
        pair_s[...] = jnp.zeros_like(pair_s)
    for i in range(2):
        c_s[i] = own[i]
        c_s[2 + i] = oth[i]
    for t in (0, 2):
        panel_pair(t, c_s, f_s, fh, fl, modes, scale)
    corner_pair(0, fh, fl, a_s)
    corner_pair(2, fh, fl, a_out)
    a_out[...] += a_s[...]
    target = gr if first else pair_s
    for t in range(2):
        for part in block_parts(t, c_s, fh, fl, lr, rr, lc, rc, target, gc, gt, modes):
            part()
    if not first:
        gr[...] = gr_in[...] + pair_s[...]


def early(own, oth, tables, rest, first, modes, scale, cost):
    lr, rr, lc, rc = tables
    row_pad, col_pad = lr.shape[0], lc.shape[0]
    n = own.shape[2]
    vmem = pl.BlockSpec(memory_space=pltpu.VMEM)
    smem = pl.BlockSpec(memory_space=pltpu.SMEM)
    scratch = [
        pltpu.VMEM((4, modes, n), F32),
        pltpu.VMEM((2, PANEL, n), F32),
        pltpu.VMEM((4, PANEL, n), BF16),
        pltpu.VMEM((4, PANEL, n), BF16),
        pltpu.VMEM((PANEL, PANEL), F32),
    ]
    if not first:
        scratch.append(pltpu.VMEM((row_pad, PANEL), F32))
    shapes = [(PANEL, PANEL), (row_pad, PANEL), (col_pad, PANEL), (row_pad, col_pad)]
    return pl.pallas_call(
        functools.partial(early_kernel, modes, scale, first, False),
        in_specs=[vmem] * 6 + ([smem, vmem, vmem] if first else [vmem] * 3),
        out_specs=[vmem] * 4,
        out_shape=[jax.ShapeDtypeStruct(s, F32) for s in shapes],
        scratch_shapes=scratch,
        compiler_params=pltpu.CompilerParams(vmem_limit_bytes=32 * 2**20),
        cost_estimate=pl.CostEstimate(flops=cost, bytes_accessed=2**22, transcendentals=0),
        name="early_first" if first else "early_second",
    )(own, oth, lr, rr, lc, rc, *rest)


LATE = 12


def main_kernel(modes, scale, scal, own, oth_a, oth_b, oth, lr, rr, lc, rc, ridge_panel, a0, a1, gr_in, gc_in, gt_in,
                tile_out, rows_out,
                c_s, f_s, fh, fl, a_p, a_s, s_s, e_s, u_s, inv_s, low_s, gr, gc, gt, pr, pc):
    first_row, first_col = scal[0], scal[1]
    for i in range(4):
        c_s[i] = own[i]
        c_s[8 + i] = oth[i]
    for i in range(2):
        c_s[4 + i] = oth_a[i]
        c_s[6 + i] = oth_b[i]

    def corner_body(i, carry):
        t = 2 * (i % 2) + 8 * (i // 2)
        panel_pair(t, c_s, f_s, fh, fl, modes, scale)
        corner_pair(t, fh, fl, a_p.at[i])
        return carry

    lax.fori_loop(0, 4, corner_body, 0)
    total = (a0[...] + a1[...]) + ((a_p[0] + a_p[2]) + (a_p[1] + a_p[3]))
    a_s[...] = total + diagonal(a_s.shape, 0, 0, ridge_panel[...])
    for t in (4, 6):
        panel_pair(t, c_s, f_s, fh, fl, modes, scale)
    gr[...] = jnp.zeros_like(gr)
    gc[...] = gc_in[...]
    gt[...] = gt_in[...]
    e_s[...] = jnp.zeros_like(e_s)

    def block_body(k, carry):
        parts = []
        for b in range(3):
            t = 3 * k + b
            parts += block_parts(t, c_s, fh, fl, lr, rr, lc, rc, gr.at[t // 2], gc, gt, modes)
        slots = [[] for _ in range(16)]
        for i, part in enumerate(parts):
            slots[i * 16 // len(parts)].append(part)

        def between(i):
            for part in slots[i]:
                part()

        factor_block(k, a_s, s_s, e_s, u_s, inv_s, low_s, between)
        return carry

    lax.fori_loop(0, 4, block_body, 0)

    inverses = [pair_inverse(p, inv_s, low_s) for p in range(2)]
    cross = split(jnp.concatenate([u_s[0, :, HALF:], u_s[1, :, BLOCK : BLOCK + HALF]], 0))
    rows_gram = (gr_in[...] + (gr[0] + gr[1])) + ((gr[2] + gr[3]) + (gr[4] + gr[5]))
    rows_gram = rows_gram + diagonal(rows_gram.shape, first_row, 0, ridge_panel[...])
    solve_rows(rows_gram, inverses, cross, pr)
    solve_rows(gc, inverses, cross, pc)

    rows, cols = tile_out.shape
    total = gt[...]
    ri = first_row + lax.broadcasted_iota(jnp.int32, total.shape, 0)
    ci = first_col + lax.broadcasted_iota(jnp.int32, total.shape, 1)
    update = dot3(split(pr[...]), split(pc[...]))
    total = jnp.where((ri >= PANEL) & (ci >= PANEL), total - update, total)
    tile_out[...] = total[0:rows, 0:cols]
    line = first_row + lax.broadcasted_iota(jnp.int32, (rows, PANEL), 0)
    at = lax.broadcasted_iota(jnp.int32, (rows, PANEL), 1)
    rows_out[...] = jnp.where(at <= line, pr[0:rows, :], 0.0)


def main(scal, own, oth_a, oth_b, oth, tables, ridge_panel, sums, rows, cols, scale):
    modes, n = own.shape[1:]
    lr, rr, lc, rc = tables
    row_pad, col_pad = lr.shape[0], lc.shape[0]
    vmem = pl.BlockSpec(memory_space=pltpu.VMEM)
    return pl.pallas_call(
        functools.partial(main_kernel, modes, scale),
        in_specs=[pl.BlockSpec(memory_space=pltpu.SMEM)] + [vmem] * 14,
        out_specs=[vmem, vmem],
        out_shape=[jax.ShapeDtypeStruct((rows, cols), F32), jax.ShapeDtypeStruct((rows, PANEL), F32)],
        scratch_shapes=[
            pltpu.VMEM((LATE, modes, n), F32),
            pltpu.VMEM((2, PANEL, n), F32),
            pltpu.VMEM((LATE, PANEL, n), BF16),
            pltpu.VMEM((LATE, PANEL, n), BF16),
            pltpu.VMEM((4, PANEL, PANEL), F32),
            pltpu.VMEM((PANEL, PANEL), F32),
            pltpu.VMEM((BLOCK, 2 * BLOCK), F32),
            pltpu.VMEM((BLOCK, BLOCK), F32),
            pltpu.VMEM((4, BLOCK, PANEL), F32),
            pltpu.VMEM((4, BLOCK, BLOCK), F32),
            pltpu.VMEM((4, BLOCK, BLOCK), F32),
            pltpu.VMEM((LATE // 2, row_pad, PANEL), F32),
            pltpu.VMEM((col_pad, PANEL), F32),
            pltpu.VMEM((row_pad, col_pad), F32),
            pltpu.VMEM((row_pad, PANEL), F32),
            pltpu.VMEM((col_pad, PANEL), F32),
        ],
        compiler_params=pltpu.CompilerParams(vmem_limit_bytes=44 * 2**20),
        name="gram_factor",
    )(scal, own, oth_a, oth_b, oth, lr, rr, lc, rc, ridge_panel, *sums)


def swap(value, axis, bit):
    size = lax.axis_size(axis)
    return lax.ppermute(value, axis, [(i, i ^ bit) for i in range(size)])


def padded(count):
    return -(-count // 16) * 16


def per_device(snapshots, pod_basis, reference_field, ridge_weights):
    contract = (((1,), (1,)), ((), ()))
    modes = pod_basis.shape[0]
    snap_total = snapshots.shape[0] * lax.axis_size("snap")
    scale = snap_total**-0.5
    feature_total = ridge_weights.shape[0]
    rows = feature_total // lax.axis_size("cells")
    cols = feature_total // lax.axis_size("snap")
    group = lax.axis_index("snap")
    core = lax.axis_index("cells") & 1
    first_row = lax.axis_index("cells") * rows
    first_col = group * cols
    scal = jnp.stack([first_row, first_col]).astype(jnp.int32)
    tables = picks(scal, padded(rows), padded(cols), modes, scale)
    ridge_panel = ridge_weights[None, :PANEL]
    ridge_cols = lax.dynamic_slice_in_dim(ridge_weights, first_col, cols)
    ridge_cols = jnp.pad(ridge_cols, (0, padded(cols) - cols))[None, :]

    projected = lax.dot_general(pod_basis, snapshots, contract, preferred_element_type=F32)
    offset = lax.dot_general(pod_basis, reference_field[None, :], contract, preferred_element_type=F32)
    partial = projected - offset

    half = partial.shape[1] // 2
    keep = lax.dynamic_slice_in_dim(partial, core * half, half, 1)
    send = lax.dynamic_slice_in_dim(partial, (1 - core) * half, half, 1)
    total = keep + swap(send, "cells", 1)
    for bit in (2, 4, 8):
        total = total + swap(total, "cells", bit)

    together = lax.optimization_barrier
    own0 = total[None]
    own1 = swap(own0, "snap", 4)
    oth0 = swap(own0, "cells", 1)
    own1, oth0, tables, ridge_panel, ridge_cols = together((own1, oth0, tables, ridge_panel, ridge_cols))
    pair = jnp.concatenate([own0, own1], 0)
    own2 = swap(pair, "snap", 2)
    oth_pair = jnp.concatenate([oth0, swap(own1, "cells", 1)], 0)
    sums = early(pair, oth_pair, tables, (scal, ridge_panel, ridge_cols), True, modes, scale, 2 * 10**9)
    own2, oth_pair, a0, gr, gc, gt = together((own2, oth_pair, *sums))
    own3 = swap(jnp.concatenate([pair, own2], 0), "snap", 1)
    oth2 = swap(own2, "cells", 1)
    sums = early(own2, oth2, tables, (gr, gc, gt), False, modes, scale, 2 * 10**9)
    own3, oth2, a1, gr, gc, gt = together((own3, oth2, *sums))
    oth3 = swap(own3, "cells", 1)
    sums = (a0, a1, gr, gc, gt)
    return tuple(main(scal, own3, oth_pair, oth2, oth3, tables, ridge_panel, sums, rows, cols, scale))


def solution(mesh):
    return jax.shard_map(
        per_device,
        mesh=mesh,
        in_specs=(P("snap", "cells"), P(None, "cells"), P("cells"), P()),
        out_specs=(P("cells", "snap"), P("cells", None)),
        check_vma=False,
    )
```

```python
import functools
import jax
import jax.numpy as jnp
import numpy as np
from jax import lax
from jax.experimental import pallas as pl
from jax.experimental.pallas import tpu as pltpu
from jax.sharding import PartitionSpec as P

PANEL = 512
HI = lax.Precision.HIGHEST
HALF = 256
BLOCK = 128
STEP = 32
SLOTS = 112
F32 = jnp.float32
BF16 = jnp.bfloat16
NT = (((1,), (1,)), ((), ()))
TN = (((0,), (0,)), ((), ()))
NN = (((1,), (0,)), ((), ()))


def dot(a, b, dims, precision=None):
    return lax.dot_general(a, b, dims, precision=precision, preferred_element_type=F32)


def split(value):
    high = value.astype(BF16)
    return high, (value - high.astype(F32)).astype(BF16)


def dot3(a, b):
    ah, al = a
    bh, bl = b
    return dot(jnp.concatenate([ah, ah, al], 1), jnp.concatenate([bh, bl, bh], 1), NT)


def pick_tables(first, rows, modes):
    index = first + lax.broadcasted_iota(jnp.int32, (rows, 128), 0)
    slot = lax.broadcasted_iota(jnp.int32, (rows, 128), 1)

    def offset(a):
        return modes + modes * a - (a * (a - 1)) // 2

    linear = index < modes
    here = (index >= offset(slot)) & (index < offset(slot + 1)) & (slot < modes)
    right_value = jnp.where(here, index - offset(slot) + slot, 0).astype(F32)
    right_index = jnp.sum(right_value, axis=1, keepdims=True).astype(jnp.int32)
    left_index = jnp.sum(jnp.where(here, slot, 0).astype(F32), axis=1, keepdims=True).astype(jnp.int32)
    left_index = jnp.where(linear, index, left_index)
    right_index = jnp.where(linear, modes, right_index)
    return (slot == left_index).astype(F32), (slot == right_index).astype(F32)


def pick_kernel(modes, scale, scal, lr, rr, lc, rc):
    for ref_l, ref_r, first in ((lr, rr, scal[0]), (lc, rc, scal[1])):
        rows = ref_l.shape[0]
        left, right = pick_tables(first, rows, modes)
        left = left * scale
        for ref, value in ((ref_l, left), (ref_r, right)):
            ref[:, 0:SLOTS] = value[:, 0:SLOTS].astype(BF16)
            ref[:, SLOTS : 2 * SLOTS] = value[:, 0:SLOTS].astype(BF16)


def picks(scal, row_pad, col_pad, modes, scale):
    shapes = [(row_pad, 2 * SLOTS)] * 2 + [(col_pad, 2 * SLOTS)] * 2
    return pl.pallas_call(
        functools.partial(pick_kernel, modes, scale),
        in_specs=[pl.BlockSpec(memory_space=pltpu.SMEM)],
        out_shape=[jax.ShapeDtypeStruct(s, BF16) for s in shapes],
        compiler_params=pltpu.CompilerParams(vmem_limit_bytes=40 * 2**20),
        name="picks",
    )(scal)


def panel_features(c_ref, t, f_ref, modes, scale):
    f_ref[0:modes, :] = c_ref[t] * scale
    at, a = modes, 0
    while at < PANEL:
        count = min(modes - a, PANEL - at)
        f_ref[at : at + count, :] = c_ref[t, a : a + count, :] * (c_ref[t, a : a + 1, :] * scale)
        at += count
        a += 1


def panel_pair(t, c_s, f_s, fh, fl, modes, scale):
    for i in range(2):
        panel_features(c_s, t + i, f_s.at[i], modes, scale)
        fh[t + i], fl[t + i] = split(f_s[i])


def corner_pair(t, fh, fl, a_ref):
    pairs = [(fh[t + i], fl[t + i]) for i in range(2)]
    top = [dot3((h[0:HALF], l[0:HALF]), (h, l)) for h, l in pairs]
    low = [dot3((h[HALF:], l[HALF:]), (h[HALF:], l[HALF:])) for h, l in pairs]
    a_ref[0:HALF, :] = top[0] + top[1]
    a_ref[HALF:, HALF:] = low[0] + low[1]


def lane_bcast(x, c):
    return jnp.broadcast_to(x[:, c : c + 1], (8, 128))


def sub_bcast(x, k):
    return jnp.broadcast_to(x[k : k + 1, :], (8, 128))


def split3(value):
    high = value.astype(BF16)
    rest = value - high.astype(F32)
    middle = rest.astype(BF16)
    return high, middle, (rest - middle.astype(F32)).astype(BF16)


def update_dot(left, right):
    lh, lm, ll = split3(left)
    rh, rm, rl = split3(right)
    return dot(
        jnp.concatenate([lh, lh, lh, lm, lm, ll], 0), jnp.concatenate([rh, rm, rl, rh, rm, rh], 0), TN
    )


def factor_step(s_ref, b, between):
    lo = STEP * b
    strips = STEP // 8
    sub = lax.broadcasted_iota(jnp.int32, (8, 128), 0)
    T = [[s_ref[lo + 8 * r : lo + 8 * r + 8, 0:128], s_ref[lo + 8 * r : lo + 8 * r + 8, 128:256]] for r in range(strips)]
    B = {(r, j): lane_bcast(T[r][0], lo + j) for j in range(STEP) for r in range(j // 8, strips)}
    for q in range(strips):
        scale = None
        for k in range(8 * q, 8 * q + 8):
            rs = lax.rsqrt(sub_bcast(B[q, k], k - 8 * q))
            inv = rs * rs
            scale = rs if scale is None else jnp.where(sub == k - 8 * q, rs, scale)
            row = [sub_bcast(part, k - 8 * q) for part in T[q]]
            pivots = {j: sub_bcast(B[j // 8, k], j % 8) for j in range(k + 1, STEP)}
            for r in range(q, strips):
                m = B[r, k] * inv
                if r == q:
                    m = jnp.where(sub > k - 8 * q, m, 0.0)
                for j in range(k + 1, STEP):
                    if j // 8 <= r:
                        B[r, j] = B[r, j] - m * pivots[j]
                T[r] = [part - m * line for part, line in zip(T[r], row)]
        T[q] = [part * scale for part in T[q]]
        between(4 * b + q)
    for r in range(strips):
        s_ref[lo + 8 * r : lo + 8 * r + 8, 0:128] = T[r][0]
        s_ref[lo + 8 * r : lo + 8 * r + 8, 128:256] = T[r][1]
    if b < 3:
        full = s_ref[lo : lo + STEP, :]
        upd = update_dot(full[:, 0:128], full)
        s_ref[lo + STEP : 128, :] -= upd[lo + STEP :, :]


def factor_block(k, a_s, s_ref, e_s, u_s, inv_s, low_s, between):
    lo, hi = BLOCK * k, BLOCK * (k + 1)
    ri = lax.broadcasted_iota(jnp.int32, (BLOCK, BLOCK), 0)
    ci = lax.broadcasted_iota(jnp.int32, (BLOCK, BLOCK), 1)
    s_ref[:, 0:BLOCK] = a_s[lo:hi, lo:hi]
    s_ref[:, BLOCK:] = (ri == ci).astype(F32)
    for b in range(4):
        factor_step(s_ref, b, between)
    inverse = s_ref[:, BLOCK:]
    inv_s[k] = inverse
    if hi < PANEL:
        rest = dot(inverse, a_s[lo:hi, hi:], NN, HI)
        u_s[lo:hi, hi:] = rest
        a_s[hi : hi + BLOCK, hi:] -= dot(rest[:, 0:BLOCK], rest, TN, HI)
        if hi + BLOCK < PANEL:
            far = rest[:, BLOCK:]
            a_s[hi + BLOCK :, hi + BLOCK :] -= dot(far, far, TN, HI)
    if k % 2:
        low_s[k // 2] = dot(inverse, e_s[...], NN, HI)
    else:
        e_s[...] = -dot(rest[:, 0:BLOCK], inverse, TN, HI)


def stacked(c, modes):
    n = c.shape[1]
    high, low = split(c)
    gap = lax.broadcasted_iota(jnp.int32, (SLOTS - modes, n), 0)
    ones = (gap == 0).astype(F32).astype(BF16)
    none = jnp.zeros((SLOTS - modes, n), BF16)
    return jnp.concatenate([high, ones, low, none], axis=0)


def picked(left, right, cs):
    return split(dot(left, cs, NN) * dot(right, cs, NN))


def block_parts(t, c_s, fh, fl, lr, rr, lc, rc, gr, gc, gt, modes):
    env = {}

    def part0():
        cs = stacked(c_s[t], modes)
        env["fr"] = picked(lr[...], rr[...], cs)
        env["fc"] = picked(lc[...], rc[...], cs)
        env["fp"] = (fh[t], fl[t])

    def part1():
        gr[...] += dot3(env["fr"], env["fp"])

    def part2():
        gc[...] += dot3(env["fc"], env["fp"])

    def part3():
        gt[...] += dot3(env["fr"], env["fc"])

    return [part0, part1, part2, part3]


def pair_inverse(p, inv_s, low_s):
    zero = jnp.zeros((BLOCK, BLOCK), F32)
    top = jnp.concatenate([inv_s[2 * p], zero], 1)
    return jnp.concatenate([top, jnp.concatenate([low_s[p], inv_s[2 * p + 1]], 1)], 0)


def diagonal(shape, first_row, first_col, values):
    ri = first_row + lax.broadcasted_iota(jnp.int32, shape, 0)
    ci = first_col + lax.broadcasted_iota(jnp.int32, shape, 1)
    return jnp.where(ri == ci, values, 0.0)


def diagonal(shape, first_row, first_col, values):
    ri = first_row + lax.broadcasted_iota(jnp.int32, shape, 0)
    ci = first_col + lax.broadcasted_iota(jnp.int32, shape, 1)
    return jnp.where(ri == ci, values, 0.0)


def early_kernel(modes, scale, first, *refs):
    own, oth, lr, rr, lc, rc = refs[0:6]
    if first:
        scal, ridge_panel, ridge_cols = refs[6:9]
        a_out, gr, gc, gt, c_s, f_s, fh, fl, a_s = refs[9:]
        gr[...] = jnp.zeros_like(gr)
        gc[...] = diagonal(gc.shape, scal[1], 0, ridge_panel[...])
        gt[...] = diagonal(gt.shape, scal[0], scal[1], ridge_cols[...])
        work = [(0, gr), (1, gr)]
    else:
        left, gr_in, gc_in, gt_in = refs[6:10]
        a_out, gr, gr_oth, gc, gt, c_s, f_s, fh, fl, a_s, pair_s = refs[10:]
        gc[...] = gc_in[...]
        gt[...] = gt_in[...]
        gr_oth[...] = jnp.zeros_like(gr_oth)
        pair_s[...] = jnp.zeros_like(pair_s)
        work = [(t, pair_s.at[t // 2]) for t in range(4)] + [(4, gr_oth), (5, gr_oth)]
        for i in range(2):
            c_s[4 + i] = left[i]
        panel_pair(4, c_s, f_s, fh, fl, modes, scale)
    for i in range(2):
        c_s[i] = own[i]
        c_s[2 + i] = oth[i]
    for t in (0, 2):
        panel_pair(t, c_s, f_s, fh, fl, modes, scale)
    corner_pair(0, fh, fl, a_s)
    corner_pair(2, fh, fl, a_out)
    a_out[...] += a_s[...]
    for t, target in work:
        for part in block_parts(t, c_s, fh, fl, lr, rr, lc, rc, target, gc, gt, modes):
            part()
    if not first:
        gr[...] = gr_in[...] + pair_s[0]
        gr_oth[...] += pair_s[1]


def early(own, oth, tables, rest, first, modes, scale, cost):
    lr, rr, lc, rc = tables
    row_pad, col_pad = lr.shape[0], lc.shape[0]
    n = own.shape[2]
    vmem = pl.BlockSpec(memory_space=pltpu.VMEM)
    smem = pl.BlockSpec(memory_space=pltpu.SMEM)
    held = 4 if first else 6
    scratch = [
        pltpu.VMEM((held, modes, n), F32),
        pltpu.VMEM((2, PANEL, n), F32),
        pltpu.VMEM((held, PANEL, n), BF16),
        pltpu.VMEM((held, PANEL, n), BF16),
        pltpu.VMEM((PANEL, PANEL), F32),
    ]
    if not first:
        scratch.append(pltpu.VMEM((2, row_pad, PANEL), F32))
    shapes = [(PANEL, PANEL)] + [(row_pad, PANEL)] * (1 if first else 2) + [(col_pad, PANEL), (row_pad, col_pad)]
    return pl.pallas_call(
        functools.partial(early_kernel, modes, scale, first),
        in_specs=[vmem] * 6 + ([smem, vmem, vmem] if first else [vmem] * 4),
        out_specs=[vmem] * len(shapes),
        out_shape=[jax.ShapeDtypeStruct(s, F32) for s in shapes],
        scratch_shapes=scratch,
        compiler_params=pltpu.CompilerParams(vmem_limit_bytes=32 * 2**20),
        cost_estimate=pl.CostEstimate(flops=cost, bytes_accessed=2**22, transcendentals=0),
        name="early_first" if first else "early_second",
    )(own, oth, lr, rr, lc, rc, *rest)


def corner_kernel(modes, scale, c_ref, a_out, fh, fl, f_s):
    for i in range(2):
        panel_pair(2 * i, c_ref, f_s, fh, fl, modes, scale)
        corner_pair(2 * i, fh, fl, a_out.at[i])


def corner_of(own, modes, scale):
    n = own.shape[2]
    vmem = pl.BlockSpec(memory_space=pltpu.VMEM)
    return pl.pallas_call(
        functools.partial(corner_kernel, modes, scale),
        in_specs=[vmem],
        out_specs=[vmem] * 3,
        out_shape=[
            jax.ShapeDtypeStruct((2, PANEL, PANEL), F32),
            jax.ShapeDtypeStruct((4, PANEL, n), BF16),
            jax.ShapeDtypeStruct((4, PANEL, n), BF16),
        ],
        scratch_shapes=[pltpu.VMEM((2, PANEL, n), F32)],
        compiler_params=pltpu.CompilerParams(vmem_limit_bytes=24 * 2**20),
        cost_estimate=pl.CostEstimate(flops=10**9, bytes_accessed=2**22, transcendentals=0),
        name="late_corner",
    )(own)


def halves_kernel(core_ref, part, offset, keep, send):
    core = core_ref[0]
    half = keep.shape[1]
    mine = pl.multiple_of(core * half, half)
    other = pl.multiple_of((1 - core) * half, half)
    send[...] = (part[pl.ds(other, half), :] - offset[...]).T
    keep[...] = (part[pl.ds(mine, half), :] - offset[...]).T


def halves(core, part, offset):
    vmem = pl.BlockSpec(memory_space=pltpu.VMEM)
    snaps, modes = part.shape
    return pl.pallas_call(
        halves_kernel,
        in_specs=[pl.BlockSpec(memory_space=pltpu.SMEM)] + [vmem] * 2,
        out_specs=[vmem] * 2,
        out_shape=[jax.ShapeDtypeStruct((modes, snaps // 2), F32)] * 2,
        compiler_params=pltpu.CompilerParams(vmem_limit_bytes=16 * 2**20),
        name="halves",
    )(core, part, offset)


LATE = 8


def main_kernel(modes, scale, scal, own, oth, lr, rr, lc, rc, ridge_panel,
                own_h, own_l, a_own, a0, a1, gr_in, gr_oth_in, gc_in, gt_in,
                tile_out, rows_out,
                f_s, fh, fl, a_p, a_s, s_s, e_s, u_s, inv_s, low_s, gr, gc, gt, pr, pc):
    first_row, first_col = scal[0], scal[1]
    rows, cols = tile_out.shape

    def corner_body(i, carry):
        panel_pair(2 * i, oth, f_s, fh, fl, modes, scale)
        corner_pair(2 * i, fh, fl, a_p.at[i])
        return carry

    lax.fori_loop(0, 2, corner_body, 0)
    total = (a0[...] + a1[...]) + ((a_own[0] + a_p[0]) + (a_own[1] + a_p[1]))
    a_s[...] = total + diagonal(a_s.shape, 0, 0, ridge_panel[...])
    gr[...] = jnp.zeros_like(gr)
    gc[...] = gc_in[...]
    gt[...] = gt_in[...]

    parts = []
    for t in range(LATE):
        held = (own, own_h, own_l) if t < 4 else (oth, fh, fl)
        parts += block_parts(t % 4, *held, lr, rr, lc, rc, gr.at[t // 2], gc, gt, modes)

    def solve_first():
        inverse = pair_inverse(0, inv_s, low_s)
        cross = u_s[0:HALF, HALF:]
        line = diagonal(pr.shape, first_row, 0, ridge_panel[...])
        sums = (gr_in[...] + (gr[0] + gr[1])) + (gr_oth_in[...] + (gr[2] + gr[3])) + line
        for p, g in ((pr, sums), (pc, gc[...])):
            first = dot(g[:, 0:HALF], inverse, NT, HI)
            p[:, 0:HALF] = first
            p[:, HALF:] = g[:, HALF:] - dot(first, cross, NN, HI)

    def update(at):
        ri = first_row + lax.broadcasted_iota(jnp.int32, gt.shape, 0)
        ci = first_col + lax.broadcasted_iota(jnp.int32, gt.shape, 1)
        change = dot3(split(pr[:, at : at + HALF]), split(pc[:, at : at + HALF]))
        return gt[...] - jnp.where((ri >= PANEL) & (ci >= PANEL), change, 0.0)

    def write_rows(at):
        line = first_row + lax.broadcasted_iota(jnp.int32, (rows, HALF), 0)
        place = at + lax.broadcasted_iota(jnp.int32, (rows, HALF), 1)
        rows_out[:, at : at + HALF] = jnp.where(place <= line, pr[0:rows, at : at + HALF], 0.0)

    def update_first():
        gt[...] = update(0)
        write_rows(0)

    slots = [[] for _ in range(64)]
    for i, part in enumerate(parts):
        slots[i * 48 // len(parts)].append(part)
    slots[49].append(solve_first)
    slots[54].append(update_first)

    def between_of(k):
        def between(i):
            for part in slots[16 * k + i]:
                part()

        return between

    for k in range(4):
        factor_block(k, a_s, s_s, e_s, u_s, inv_s, low_s, between_of(k))

    inverse = pair_inverse(1, inv_s, low_s)
    for p in (pr, pc):
        p[:, HALF:] = dot(p[:, HALF:], inverse, NT, HI)
    tile_out[...] = update(HALF)[0:rows, 0:cols]
    write_rows(HALF)


def main(scal, own, oth, tables, ridge_panel, sums, rows, cols, scale):
    modes, n = own.shape[1:]
    lr, rr, lc, rc = tables
    row_pad, col_pad = lr.shape[0], lc.shape[0]
    vmem = pl.BlockSpec(memory_space=pltpu.VMEM)
    return pl.pallas_call(
        functools.partial(main_kernel, modes, scale),
        in_specs=[pl.BlockSpec(memory_space=pltpu.SMEM)] + [vmem] * 16,
        out_specs=[vmem, vmem],
        out_shape=[jax.ShapeDtypeStruct((rows, cols), F32), jax.ShapeDtypeStruct((rows, PANEL), F32)],
        scratch_shapes=[
            pltpu.VMEM((2, PANEL, n), F32),
            pltpu.VMEM((4, PANEL, n), BF16),
            pltpu.VMEM((4, PANEL, n), BF16),
            pltpu.VMEM((2, PANEL, PANEL), F32),
            pltpu.VMEM((PANEL, PANEL), F32),
            pltpu.VMEM((BLOCK, 2 * BLOCK), F32),
            pltpu.VMEM((BLOCK, BLOCK), F32),
            pltpu.VMEM((PANEL, PANEL), F32),
            pltpu.VMEM((4, BLOCK, BLOCK), F32),
            pltpu.VMEM((2, BLOCK, BLOCK), F32),
            pltpu.VMEM((LATE // 2, row_pad, PANEL), F32),
            pltpu.VMEM((col_pad, PANEL), F32),
            pltpu.VMEM((row_pad, col_pad), F32),
            pltpu.VMEM((row_pad, PANEL), F32),
            pltpu.VMEM((col_pad, PANEL), F32),
        ],
        compiler_params=pltpu.CompilerParams(vmem_limit_bytes=32 * 2**20),
        name="gram_factor",
    )(scal, own, oth, lr, rr, lc, rc, ridge_panel, *sums)


def swap(value, axis, bit, other_bit=None):
    size = lax.axis_size(axis)
    bits = (bit, bit if other_bit is None else other_bit)
    return lax.ppermute(value, axis, [(i, i ^ bits[i & 1]) for i in range(size)])


def padded(count):
    return -(-count // 16) * 16


def per_device(snapshots, pod_basis, reference_field, ridge_weights):
    modes = pod_basis.shape[0]
    snap_total = snapshots.shape[0] * lax.axis_size("snap")
    scale = snap_total**-0.5
    feature_total = ridge_weights.shape[0]
    rows = feature_total // lax.axis_size("cells")
    cols = feature_total // lax.axis_size("snap")
    group = lax.axis_index("snap")
    core = lax.axis_index("cells") & 1
    first_row = lax.axis_index("cells") * rows
    first_col = group * cols
    scal = jnp.stack([first_row, first_col]).astype(jnp.int32)
    tables = picks(scal, padded(rows), padded(cols), modes, scale)
    ridge_panel = ridge_weights[None, :PANEL]
    ridge_cols = lax.dynamic_slice_in_dim(ridge_weights, first_col, cols)
    ridge_cols = jnp.pad(ridge_cols, (0, padded(cols) - cols))[None, :]

    projected = lax.dot_general(snapshots, pod_basis, NT, preferred_element_type=F32)
    offset = lax.dot_general(reference_field[None, :], pod_basis, NT, preferred_element_type=F32)
    keep, send = halves(core[None].astype(jnp.int32), projected, offset)
    total = keep + swap(send, "cells", 1)
    for bit, other_bit in ((2, 4), (4, 2), (8, 8)):
        total = total + swap(total, "cells", bit, other_bit)

    together = lax.optimization_barrier
    own0 = total[None]
    own1 = swap(own0, "snap", 4)
    oth0 = swap(own0, "cells", 1)
    own1, oth0, tables, ridge_panel, ridge_cols = together((own1, oth0, tables, ridge_panel, ridge_cols))
    pair = jnp.concatenate([own0, own1], 0)
    own2 = swap(pair, "snap", 2)
    oth_pair = jnp.concatenate([oth0, swap(own1, "cells", 1)], 0)
    sums = early(pair, oth_pair, tables, (scal, ridge_panel, ridge_cols), True, modes, scale, 4 * 10**9)
    own2, a0, *sums = together((own2, *sums))
    own3 = swap(jnp.concatenate([pair, own2], 0), "snap", 1)
    oth2 = swap(own2, "cells", 1)
    sums = early(own2, oth2, tables, (oth_pair, *sums), False, modes, scale, 4 * 10**9)
    own3, a1, *sums = together((own3, *sums))
    oth3 = swap(own3, "cells", 1)
    a_own, own_h, own_l = corner_of(own3, modes, scale)
    oth3, a_own, own_h, own_l = together((oth3, a_own, own_h, own_l))
    given = (own_h, own_l, a_own, a0, a1, *sums)
    return tuple(main(scal, own3, oth3, tables, ridge_panel, given, rows, cols, scale))


def solution(mesh):
    return jax.shard_map(
        per_device,
        mesh=mesh,
        in_specs=(P("snap", "cells"), P(None, "cells"), P("cells"), P()),
        out_specs=(P("cells", "snap"), P("cells", None)),
        check_vma=False,
    )
```

```python
import functools
import math

import jax
import jax.numpy as jnp
import numpy as np
from jax import lax
from jax.experimental import pallas as pl
from jax.experimental.pallas import tpu as pltpu
from jax.sharding import PartitionSpec as P

PANEL = 512
HI = lax.Precision.HIGHEST
HALF = 256
BLOCK = 128
STEP = 32
SLOTS = 112
F32 = jnp.float32
BF16 = jnp.bfloat16
NT = (((1,), (1,)), ((), ()))
TN = (((0,), (0,)), ((), ()))
NN = (((1,), (0,)), ((), ()))


def dot(a, b, dims, precision=None):
    return lax.dot_general(a, b, dims, precision=precision, preferred_element_type=F32)


def split(value):
    high = value.astype(BF16)
    return high, (value - high.astype(F32)).astype(BF16)


def dot3(a, b):
    ah, al = a
    bh, bl = b
    return dot(jnp.concatenate([ah, ah, al], 1), jnp.concatenate([bh, bl, bh], 1), NT)


def pick_tables(first, rows, modes):
    index = first + lax.broadcasted_iota(jnp.int32, (rows, 128), 0)
    slot = lax.broadcasted_iota(jnp.int32, (rows, 128), 1)

    def offset(a):
        return modes + modes * a - (a * (a - 1)) // 2

    linear = index < modes
    here = (index >= offset(slot)) & (index < offset(slot + 1)) & (slot < modes)
    right_value = jnp.where(here, index - offset(slot) + slot, 0).astype(F32)
    right_index = jnp.sum(right_value, axis=1, keepdims=True).astype(jnp.int32)
    left_index = jnp.sum(jnp.where(here, slot, 0).astype(F32), axis=1, keepdims=True).astype(jnp.int32)
    left_index = jnp.where(linear, index, left_index)
    right_index = jnp.where(linear, modes, right_index)
    return (slot == left_index).astype(F32), (slot == right_index).astype(F32)


def pick_kernel(modes, scale, scal, lr, rr, lc, rc):
    for ref_l, ref_r, first in ((lr, rr, scal[0]), (lc, rc, scal[1])):
        block = math.gcd(lr.shape[0], ref_l.shape[0])

        def rows_body(i, carry, ref_l=ref_l, ref_r=ref_r, first=first):
            at = pl.ds(pl.multiple_of(i * block, 16), block)
            left, right = pick_tables(first + i * block, block, modes)
            for ref, value in ((ref_l, left * scale), (ref_r, right)):
                ref[at, 0:SLOTS] = value[:, 0:SLOTS].astype(BF16)
                ref[at, SLOTS : 2 * SLOTS] = value[:, 0:SLOTS].astype(BF16)
            return carry

        lax.fori_loop(0, ref_l.shape[0] // block, rows_body, 0)


def picks(scal, row_pad, col_pad, modes, scale):
    shapes = [(row_pad, 2 * SLOTS)] * 2 + [(col_pad, 2 * SLOTS)] * 2
    return pl.pallas_call(
        functools.partial(pick_kernel, modes, scale),
        in_specs=[pl.BlockSpec(memory_space=pltpu.SMEM)],
        out_shape=[jax.ShapeDtypeStruct(s, BF16) for s in shapes],
        compiler_params=pltpu.CompilerParams(vmem_limit_bytes=40 * 2**20),
        name="picks",
    )(scal)


def panel_features(c_ref, t, f_ref, modes, scale):
    f_ref[0:modes, :] = c_ref[t] * scale
    at, a = modes, 0
    while at < PANEL:
        count = min(modes - a, PANEL - at)
        f_ref[at : at + count, :] = c_ref[t, a : a + count, :] * (c_ref[t, a : a + 1, :] * scale)
        at += count
        a += 1


def panel_pair(t, c_s, f_s, fh, fl, modes, scale):
    for i in range(2):
        panel_features(c_s, t + i, f_s.at[i], modes, scale)
        fh[t + i], fl[t + i] = split(f_s[i])


def corner_pair(t, fh, fl, a_ref):
    pairs = [(fh[t + i], fl[t + i]) for i in range(2)]
    top = [dot3((h[0:HALF], l[0:HALF]), (h, l)) for h, l in pairs]
    low = [dot3((h[HALF:], l[HALF:]), (h[HALF:], l[HALF:])) for h, l in pairs]
    a_ref[0:HALF, :] = top[0] + top[1]
    a_ref[HALF:, HALF:] = low[0] + low[1]


def lane_bcast(x, c):
    return jnp.broadcast_to(x[:, c : c + 1], (8, 128))


def sub_bcast(x, k):
    return jnp.broadcast_to(x[k : k + 1, :], (8, 128))


def split3(value):
    high = value.astype(BF16)
    rest = value - high.astype(F32)
    middle = rest.astype(BF16)
    return high, middle, (rest - middle.astype(F32)).astype(BF16)


def update_dot(left, right):
    lh, lm, ll = split3(left)
    rh, rm, rl = split3(right)
    return dot(
        jnp.concatenate([lh, lh, lh, lm, lm, ll], 0), jnp.concatenate([rh, rm, rl, rh, rm, rh], 0), TN
    )


def factor_step(s_ref, b, between):
    lo = STEP * b
    strips = STEP // 8
    sub = lax.broadcasted_iota(jnp.int32, (8, 128), 0)
    T = [[s_ref[lo + 8 * r : lo + 8 * r + 8, 0:128], s_ref[lo + 8 * r : lo + 8 * r + 8, 128:256]] for r in range(strips)]
    B = {(r, j): lane_bcast(T[r][0], lo + j) for j in range(STEP) for r in range(j // 8, strips)}
    for q in range(strips):
        scale = None
        for k in range(8 * q, 8 * q + 8):
            rs = lax.rsqrt(sub_bcast(B[q, k], k - 8 * q))
            inv = rs * rs
            scale = rs if scale is None else jnp.where(sub == k - 8 * q, rs, scale)
            row = [sub_bcast(part, k - 8 * q) for part in T[q]]
            pivots = {j: sub_bcast(B[j // 8, k], j % 8) for j in range(k + 1, STEP)}
            for r in range(q, strips):
                m = B[r, k] * inv
                if r == q:
                    m = jnp.where(sub > k - 8 * q, m, 0.0)
                for j in range(k + 1, STEP):
                    if j // 8 <= r:
                        B[r, j] = B[r, j] - m * pivots[j]
                T[r] = [part - m * line for part, line in zip(T[r], row)]
        T[q] = [part * scale for part in T[q]]
        between(4 * b + q)
    for r in range(strips):
        s_ref[lo + 8 * r : lo + 8 * r + 8, 0:128] = T[r][0]
        s_ref[lo + 8 * r : lo + 8 * r + 8, 128:256] = T[r][1]
    if b < 3:
        full = s_ref[lo : lo + STEP, :]
        upd = update_dot(full[:, 0:128], full)
        s_ref[lo + STEP : 128, :] -= upd[lo + STEP :, :]


def factor_block(k, a_s, s_ref, e_s, u_s, inv_s, low_s, between):
    lo, hi = BLOCK * k, BLOCK * (k + 1)
    ri = lax.broadcasted_iota(jnp.int32, (BLOCK, BLOCK), 0)
    ci = lax.broadcasted_iota(jnp.int32, (BLOCK, BLOCK), 1)
    s_ref[:, 0:BLOCK] = a_s[lo:hi, lo:hi]
    s_ref[:, BLOCK:] = (ri == ci).astype(F32)
    for b in range(4):
        factor_step(s_ref, b, between)
    inverse = s_ref[:, BLOCK:]
    inv_s[k] = inverse
    if hi < PANEL:
        rest = dot(inverse, a_s[lo:hi, hi:], NN, HI)
        u_s[lo:hi, hi:] = rest
        a_s[hi : hi + BLOCK, hi:] -= dot(rest[:, 0:BLOCK], rest, TN, HI)
        if hi + BLOCK < PANEL:
            far = rest[:, BLOCK:]
            a_s[hi + BLOCK :, hi + BLOCK :] -= dot(far, far, TN, HI)
    if k % 2:
        low_s[k // 2] = dot(inverse, e_s[...], NN, HI)
    else:
        e_s[...] = -dot(rest[:, 0:BLOCK], inverse, TN, HI)


def stacked(c, modes):
    n = c.shape[1]
    high, low = split(c)
    gap = lax.broadcasted_iota(jnp.int32, (SLOTS - modes, n), 0)
    ones = (gap == 0).astype(F32).astype(BF16)
    none = jnp.zeros((SLOTS - modes, n), BF16)
    return jnp.concatenate([high, ones, low, none], axis=0)


def picked(left, right, cs):
    return split(dot(left, cs, NN) * dot(right, cs, NN))


def block_parts(t, c_s, fh, fl, lr, rr, lc, rc, gr, gc, gt, modes):
    env = {}

    def part0():
        cs = stacked(c_s[t], modes)
        env["fr"] = picked(lr[...], rr[...], cs)
        env["fc"] = picked(lc[...], rc[...], cs)
        env["fp"] = (fh[t], fl[t])

    def part1():
        gr[...] += dot3(env["fr"], env["fp"])

    def part2():
        gc[...] += dot3(env["fc"], env["fp"])

    def part3():
        gt[...] += dot3(env["fr"], env["fc"])

    return [part0, part1, part2, part3]


def pair_inverse(p, inv_s, low_s):
    zero = jnp.zeros((BLOCK, BLOCK), F32)
    top = jnp.concatenate([inv_s[2 * p], zero], 1)
    return jnp.concatenate([top, jnp.concatenate([low_s[p], inv_s[2 * p + 1]], 1)], 0)


def diagonal(shape, first_row, first_col, values):
    ri = first_row + lax.broadcasted_iota(jnp.int32, shape, 0)
    ci = first_col + lax.broadcasted_iota(jnp.int32, shape, 1)
    return jnp.where(ri == ci, values, 0.0)


def diagonal(shape, first_row, first_col, values):
    ri = first_row + lax.broadcasted_iota(jnp.int32, shape, 0)
    ci = first_col + lax.broadcasted_iota(jnp.int32, shape, 1)
    return jnp.where(ri == ci, values, 0.0)


def early_kernel(modes, scale, first, *refs):
    own, oth, lr, rr, lc, rc = refs[0:6]
    if first:
        scal, ridge_panel, ridge_cols = refs[6:9]
        a_out, gr, gc, gt, c_s, f_s, fh, fl, a_s, pair_s = refs[9:]
        pair_s[...] = jnp.zeros_like(pair_s)
        gc[...] = diagonal(gc.shape, scal[1], 0, ridge_panel[...])
        gt[...] = diagonal(gt.shape, scal[0], scal[1], ridge_cols[...])
    else:
        left, gr_in, gc_in, gt_in = refs[6:10]
        a_out, gr, gr_oth, gc, gt, c_s, f_s, fh, fl, a_s, pair_s = refs[10:]
        gc[...] = gc_in[...]
        gt[...] = gt_in[...]
        pair_s[...] = jnp.zeros_like(pair_s)
        for i in range(2):
            c_s[4 + i] = left[i]
        panel_pair(4, c_s, f_s, fh, fl, modes, scale)
    for i in range(2):
        c_s[i] = own[i]
        c_s[2 + i] = oth[i]

    def corner_body(i, carry):
        panel_pair(2 * i, c_s, f_s, fh, fl, modes, scale)
        corner_pair(2 * i, fh, fl, a_s.at[i])
        return carry

    if first:
        corner_body(0, 0)
        corner_body(1, 0)
    else:
        lax.fori_loop(0, 2, corner_body, 0)
    a_out[...] = a_s[0] + a_s[1]

    def pair_body(i, carry):
        for t in (2 * i, 2 * i + 1):
            for part in block_parts(t, c_s, fh, fl, lr, rr, lc, rc, pair_s.at[i], gc, gt, modes):
                part()
        return carry

    if first:
        pair_body(0, 0)
        gr[...] = pair_s[0]
    else:
        lax.fori_loop(0, 3, pair_body, 0)
        gr[...] = gr_in[...] + pair_s[0]
        gr_oth[...] = pair_s[2] + pair_s[1]


def early(own, oth, tables, rest, first, modes, scale, cost):
    lr, rr, lc, rc = tables
    row_pad, col_pad = lr.shape[0], lc.shape[0]
    n = own.shape[2]
    vmem = pl.BlockSpec(memory_space=pltpu.VMEM)
    smem = pl.BlockSpec(memory_space=pltpu.SMEM)
    held = 4 if first else 6
    scratch = [
        pltpu.VMEM((held, modes, n), F32),
        pltpu.VMEM((2, PANEL, n), F32),
        pltpu.VMEM((held, PANEL, n), BF16),
        pltpu.VMEM((held, PANEL, n), BF16),
        pltpu.VMEM((2, PANEL, PANEL), F32),
        pltpu.VMEM((1 if first else 3, row_pad, PANEL), F32),
    ]
    shapes = [(PANEL, PANEL)] + [(row_pad, PANEL)] * (1 if first else 2) + [(col_pad, PANEL), (row_pad, col_pad)]
    return pl.pallas_call(
        functools.partial(early_kernel, modes, scale, first),
        in_specs=[vmem] * 6 + ([smem, vmem, vmem] if first else [vmem] * 4),
        out_specs=[vmem] * len(shapes),
        out_shape=[jax.ShapeDtypeStruct(s, F32) for s in shapes],
        scratch_shapes=scratch,
        compiler_params=pltpu.CompilerParams(vmem_limit_bytes=32 * 2**20),
        cost_estimate=pl.CostEstimate(flops=cost, bytes_accessed=2**22, transcendentals=0),
        name="early_first" if first else "early_second",
    )(own, oth, lr, rr, lc, rc, *rest)


def corner_kernel(modes, scale, c_ref, a_out, fh, fl, f_s):
    for i in range(2):
        panel_pair(2 * i, c_ref, f_s, fh, fl, modes, scale)
        corner_pair(2 * i, fh, fl, a_out.at[i])


def corner_of(own, modes, scale):
    n = own.shape[2]
    vmem = pl.BlockSpec(memory_space=pltpu.VMEM)
    return pl.pallas_call(
        functools.partial(corner_kernel, modes, scale),
        in_specs=[vmem],
        out_specs=[vmem] * 3,
        out_shape=[
            jax.ShapeDtypeStruct((2, PANEL, PANEL), F32),
            jax.ShapeDtypeStruct((4, PANEL, n), BF16),
            jax.ShapeDtypeStruct((4, PANEL, n), BF16),
        ],
        scratch_shapes=[pltpu.VMEM((2, PANEL, n), F32)],
        compiler_params=pltpu.CompilerParams(vmem_limit_bytes=24 * 2**20),
        cost_estimate=pl.CostEstimate(flops=10**9, bytes_accessed=2**22, transcendentals=0),
        name="late_corner",
    )(own)


def halves_kernel(core_ref, part, offset, keep, send):
    core = core_ref[0]
    half = keep.shape[1]
    mine = pl.multiple_of(core * half, half)
    other = pl.multiple_of((1 - core) * half, half)
    send[...] = (part[pl.ds(other, half), :] - offset[...]).T
    keep[...] = (part[pl.ds(mine, half), :] - offset[...]).T


def halves(core, part, offset):
    vmem = pl.BlockSpec(memory_space=pltpu.VMEM)
    snaps, modes = part.shape
    return pl.pallas_call(
        halves_kernel,
        in_specs=[pl.BlockSpec(memory_space=pltpu.SMEM)] + [vmem] * 2,
        out_specs=[vmem] * 2,
        out_shape=[jax.ShapeDtypeStruct((modes, snaps // 2), F32)] * 2,
        compiler_params=pltpu.CompilerParams(vmem_limit_bytes=16 * 2**20),
        name="halves",
    )(core, part, offset)


LATE = 8


def main_kernel(modes, scale, scal, own, oth, lr, rr, lc, rc, ridge_panel,
                own_h, own_l, a_own, a0, a1, gr_in, gr_oth_in, gc_in, gt_in,
                tile_out, rows_out,
                f_s, fh, fl, a_p, a_s, s_s, e_s, u_s, inv_s, low_s, gr, gc, gt, pr, pc):
    first_row, first_col = scal[0], scal[1]
    rows, cols = tile_out.shape

    def corner_body(i, carry):
        panel_pair(2 * i, oth, f_s, fh, fl, modes, scale)
        corner_pair(2 * i, fh, fl, a_p.at[i])
        return carry

    lax.fori_loop(0, 2, corner_body, 0)
    total = (a0[...] + a1[...]) + ((a_own[0] + a_p[0]) + (a_own[1] + a_p[1]))
    a_s[...] = total + diagonal(a_s.shape, 0, 0, ridge_panel[...])
    gr[...] = jnp.zeros_like(gr)
    gc[...] = gc_in[...]
    gt[...] = gt_in[...]

    parts = []
    for t in range(LATE):
        held = (own, own_h, own_l) if t < 4 else (oth, fh, fl)
        parts += block_parts(t % 4, *held, lr, rr, lc, rc, gr.at[t // 2], gc, gt, modes)

    def solve_first():
        inverse = pair_inverse(0, inv_s, low_s)
        cross = u_s[0:HALF, HALF:]
        line = diagonal(pr.shape, first_row, 0, ridge_panel[...])
        sums = (gr_in[...] + (gr[0] + gr[1])) + (gr_oth_in[...] + (gr[2] + gr[3])) + line
        for p, g in ((pr, sums), (pc, gc[...])):
            first = dot(g[:, 0:HALF], inverse, NT, HI)
            p[:, 0:HALF] = first
            p[:, HALF:] = g[:, HALF:] - dot(first, cross, NN, HI)

    def update(at):
        ri = first_row + lax.broadcasted_iota(jnp.int32, gt.shape, 0)
        ci = first_col + lax.broadcasted_iota(jnp.int32, gt.shape, 1)
        change = dot3(split(pr[:, at : at + HALF]), split(pc[:, at : at + HALF]))
        return gt[...] - jnp.where((ri >= PANEL) & (ci >= PANEL), change, 0.0)

    def write_rows(at):
        line = first_row + lax.broadcasted_iota(jnp.int32, (rows, HALF), 0)
        place = at + lax.broadcasted_iota(jnp.int32, (rows, HALF), 1)
        rows_out[:, at : at + HALF] = jnp.where(place <= line, pr[0:rows, at : at + HALF], 0.0)

    def update_first():
        gt[...] = update(0)
        write_rows(0)

    slots = [[] for _ in range(64)]
    for i, part in enumerate(parts):
        slots[i * 48 // len(parts)].append(part)
    slots[49].append(solve_first)
    slots[54].append(update_first)

    def between_of(k):
        def between(i):
            for part in slots[16 * k + i]:
                part()

        return between

    for k in range(4):
        factor_block(k, a_s, s_s, e_s, u_s, inv_s, low_s, between_of(k))

    inverse = pair_inverse(1, inv_s, low_s)
    for p in (pr, pc):
        p[:, HALF:] = dot(p[:, HALF:], inverse, NT, HI)
    tile_out[...] = update(HALF)[0:rows, 0:cols]
    write_rows(HALF)


def main(scal, own, oth, tables, ridge_panel, sums, rows, cols, scale):
    modes, n = own.shape[1:]
    lr, rr, lc, rc = tables
    row_pad, col_pad = lr.shape[0], lc.shape[0]
    vmem = pl.BlockSpec(memory_space=pltpu.VMEM)
    return pl.pallas_call(
        functools.partial(main_kernel, modes, scale),
        in_specs=[pl.BlockSpec(memory_space=pltpu.SMEM)] + [vmem] * 16,
        out_specs=[vmem, vmem],
        out_shape=[jax.ShapeDtypeStruct((rows, cols), F32), jax.ShapeDtypeStruct((rows, PANEL), F32)],
        scratch_shapes=[
            pltpu.VMEM((2, PANEL, n), F32),
            pltpu.VMEM((4, PANEL, n), BF16),
            pltpu.VMEM((4, PANEL, n), BF16),
            pltpu.VMEM((2, PANEL, PANEL), F32),
            pltpu.VMEM((PANEL, PANEL), F32),
            pltpu.VMEM((BLOCK, 2 * BLOCK), F32),
            pltpu.VMEM((BLOCK, BLOCK), F32),
            pltpu.VMEM((PANEL, PANEL), F32),
            pltpu.VMEM((4, BLOCK, BLOCK), F32),
            pltpu.VMEM((2, BLOCK, BLOCK), F32),
            pltpu.VMEM((LATE // 2, row_pad, PANEL), F32),
            pltpu.VMEM((col_pad, PANEL), F32),
            pltpu.VMEM((row_pad, col_pad), F32),
            pltpu.VMEM((row_pad, PANEL), F32),
            pltpu.VMEM((col_pad, PANEL), F32),
        ],
        compiler_params=pltpu.CompilerParams(vmem_limit_bytes=32 * 2**20),
        name="gram_factor",
    )(scal, own, oth, lr, rr, lc, rc, ridge_panel, *sums)


def swap(value, axis, bit, other_bit=None):
    size = lax.axis_size(axis)
    bits = (bit, bit if other_bit is None else other_bit)
    return lax.ppermute(value, axis, [(i, i ^ bits[i & 1]) for i in range(size)])


def padded(count):
    return -(-count // 16) * 16


def per_device(snapshots, pod_basis, reference_field, ridge_weights):
    modes = pod_basis.shape[0]
    snap_total = snapshots.shape[0] * lax.axis_size("snap")
    scale = snap_total**-0.5
    feature_total = ridge_weights.shape[0]
    rows = feature_total // lax.axis_size("cells")
    cols = feature_total // lax.axis_size("snap")
    group = lax.axis_index("snap")
    core = lax.axis_index("cells") & 1
    first_row = lax.axis_index("cells") * rows
    first_col = group * cols
    scal = jnp.stack([first_row, first_col]).astype(jnp.int32)
    tables = picks(scal, padded(rows), padded(cols), modes, scale)
    ridge_panel = ridge_weights[None, :PANEL]
    ridge_cols = lax.dynamic_slice_in_dim(ridge_weights, first_col, cols)
    ridge_cols = jnp.pad(ridge_cols, (0, padded(cols) - cols))[None, :]

    projected = lax.dot_general(snapshots, pod_basis, NT, preferred_element_type=F32)
    offset = lax.dot_general(reference_field[None, :], pod_basis, NT, preferred_element_type=F32)
    keep, send = halves(core[None].astype(jnp.int32), projected, offset)
    total = keep + swap(send, "cells", 1)
    for bit, other_bit in ((2, 4), (4, 2), (8, 8)):
        total = total + swap(total, "cells", bit, other_bit)

    together = lax.optimization_barrier
    own0 = total[None]
    own1 = swap(own0, "snap", 4)
    oth0 = swap(own0, "cells", 1)
    own1, oth0, tables, ridge_panel, ridge_cols = together((own1, oth0, tables, ridge_panel, ridge_cols))
    pair = jnp.concatenate([own0, own1], 0)
    own2 = swap(pair, "snap", 2)
    oth_pair = jnp.concatenate([oth0, swap(own1, "cells", 1)], 0)
    sums = early(pair, oth_pair, tables, (scal, ridge_panel, ridge_cols), True, modes, scale, 4 * 10**9)
    own2, a0, *sums = together((own2, *sums))
    own3 = swap(jnp.concatenate([pair, own2], 0), "snap", 1)
    oth2 = swap(own2, "cells", 1)
    sums = early(own2, oth2, tables, (oth_pair, *sums), False, modes, scale, 4 * 10**9)
    own3, a1, *sums = together((own3, *sums))
    oth3 = swap(own3, "cells", 1)
    a_own, own_h, own_l = corner_of(own3, modes, scale)
    oth3, a_own, own_h, own_l = together((oth3, a_own, own_h, own_l))
    given = (own_h, own_l, a_own, a0, a1, *sums)
    return tuple(main(scal, own3, oth3, tables, ridge_panel, given, rows, cols, scale))


def solution(mesh):
    return jax.shard_map(
        per_device,
        mesh=mesh,
        in_specs=(P("snap", "cells"), P(None, "cells"), P("cells"), P()),
        out_specs=(P("cells", "snap"), P("cells", None)),
        check_vma=False,
    )
```

```python
import functools
import math

import jax
import jax.numpy as jnp
import numpy as np
from jax import lax
from jax.experimental import pallas as pl
from jax.experimental.pallas import tpu as pltpu
from jax.sharding import PartitionSpec as P

PANEL = 512
HI = lax.Precision.HIGHEST
HALF = 256
BLOCK = 128
STEP = 32
SLOTS = 112
F32 = jnp.float32
BF16 = jnp.bfloat16
NT = (((1,), (1,)), ((), ()))
TN = (((0,), (0,)), ((), ()))
NN = (((1,), (0,)), ((), ()))


def dot(a, b, dims, precision=None):
    return lax.dot_general(a, b, dims, precision=precision, preferred_element_type=F32)


def split(value):
    high = value.astype(BF16)
    return high, (value - high.astype(F32)).astype(BF16)


def dot3(a, b):
    ah, al = a
    bh, bl = b
    return dot(jnp.concatenate([ah, ah, al], 1), jnp.concatenate([bh, bl, bh], 1), NT)


def pick_tables(first, rows, modes):
    index = first + lax.broadcasted_iota(jnp.int32, (rows, 128), 0)
    slot = lax.broadcasted_iota(jnp.int32, (rows, 128), 1)

    def offset(a):
        return modes + modes * a - (a * (a - 1)) // 2

    linear = index < modes
    here = (index >= offset(slot)) & (index < offset(slot + 1)) & (slot < modes)
    right_value = jnp.where(here, index - offset(slot) + slot, 0).astype(F32)
    right_index = jnp.sum(right_value, axis=1, keepdims=True).astype(jnp.int32)
    left_index = jnp.sum(jnp.where(here, slot, 0).astype(F32), axis=1, keepdims=True).astype(jnp.int32)
    left_index = jnp.where(linear, index, left_index)
    right_index = jnp.where(linear, modes, right_index)
    return (slot == left_index).astype(F32), (slot == right_index).astype(F32)


def pick_kernel(modes, scale, scal, lr, rr, lc, rc):
    for ref_l, ref_r, first in ((lr, rr, scal[0]), (lc, rc, scal[1])):
        block = math.gcd(lr.shape[0], ref_l.shape[0])

        def rows_body(i, carry, ref_l=ref_l, ref_r=ref_r, first=first):
            at = pl.ds(pl.multiple_of(i * block, 16), block)
            left, right = pick_tables(first + i * block, block, modes)
            for ref, value in ((ref_l, left * scale), (ref_r, right)):
                ref[at, 0:SLOTS] = value[:, 0:SLOTS].astype(BF16)
                ref[at, SLOTS : 2 * SLOTS] = value[:, 0:SLOTS].astype(BF16)
            return carry

        lax.fori_loop(0, ref_l.shape[0] // block, rows_body, 0)


def picks(scal, row_pad, col_pad, modes, scale):
    shapes = [(row_pad, 2 * SLOTS)] * 2 + [(col_pad, 2 * SLOTS)] * 2
    return pl.pallas_call(
        functools.partial(pick_kernel, modes, scale),
        in_specs=[pl.BlockSpec(memory_space=pltpu.SMEM)],
        out_shape=[jax.ShapeDtypeStruct(s, BF16) for s in shapes],
        compiler_params=pltpu.CompilerParams(vmem_limit_bytes=40 * 2**20),
        name="picks",
    )(scal)


def panel_features(c_ref, t, f_ref, modes, scale):
    f_ref[0:modes, :] = c_ref[t] * scale
    at, a = modes, 0
    while at < PANEL:
        count = min(modes - a, PANEL - at)
        f_ref[at : at + count, :] = c_ref[t, a : a + count, :] * (c_ref[t, a : a + 1, :] * scale)
        at += count
        a += 1


def panel_pair(t, c_s, f_s, fh, fl, modes, scale):
    for i in range(2):
        panel_features(c_s, t + i, f_s.at[i], modes, scale)
        fh[t + i], fl[t + i] = split(f_s[i])


def corner_part(t, fh, fl, at):
    def one(i):
        h, l = fh[t + i], fl[t + i]
        rows = slice(at, at + HALF)
        return dot3((h[rows], l[rows]), (h[at:], l[at:]))

    return one(0) + one(1)


def corner_pair(t, fh, fl, a_ref):
    a_ref[0:HALF, :] = corner_part(t, fh, fl, 0)
    a_ref[HALF:, HALF:] = corner_part(t, fh, fl, HALF)


def lane_bcast(x, c):
    return jnp.broadcast_to(x[:, c : c + 1], (8, 128))


def sub_bcast(x, k):
    return jnp.broadcast_to(x[k : k + 1, :], (8, 128))


def split3(value):
    high = value.astype(BF16)
    rest = value - high.astype(F32)
    middle = rest.astype(BF16)
    return high, middle, (rest - middle.astype(F32)).astype(BF16)


def update_dot(left, right):
    lh, lm, ll = split3(left)
    rh, rm, rl = split3(right)
    return dot(
        jnp.concatenate([lh, lh, lh, lm, lm, ll], 0), jnp.concatenate([rh, rm, rl, rh, rm, rh], 0), TN
    )


def factor_step(s_ref, b, between):
    lo = STEP * b
    strips = STEP // 8
    sub = lax.broadcasted_iota(jnp.int32, (8, 128), 0)
    T = [[s_ref[lo + 8 * r : lo + 8 * r + 8, 0:128], s_ref[lo + 8 * r : lo + 8 * r + 8, 128:256]] for r in range(strips)]
    for q in range(strips):
        cols = range(8 * q, 8 * q + 8)
        B = {(r, j): lane_bcast(T[r][0], lo + j) for j in cols for r in range(q, strips)}
        scale = None
        for k in cols:
            rs = lax.rsqrt(sub_bcast(B[q, k], k - 8 * q))
            inv = rs * rs
            scale = rs if scale is None else jnp.where(sub == k - 8 * q, rs, scale)
            row = [sub_bcast(part, k - 8 * q) for part in T[q]]
            pivots = {j: sub_bcast(B[q, k], j - 8 * q) for j in range(k + 1, 8 * q + 8)}
            for r in range(q, strips):
                m = B[r, k] * inv
                if r == q:
                    m = jnp.where(sub > k - 8 * q, m, 0.0)
                for j in pivots:
                    B[r, j] = B[r, j] - m * pivots[j]
                T[r] = [part - m * line for part, line in zip(T[r], row)]
        T[q] = [part * scale for part in T[q]]
        between(4 * b + q)
    for r in range(strips):
        s_ref[lo + 8 * r : lo + 8 * r + 8, 0:128] = T[r][0]
        s_ref[lo + 8 * r : lo + 8 * r + 8, 128:256] = T[r][1]
    if b < 3:
        full = s_ref[lo : lo + STEP, :]
        upd = update_dot(full[:, 0:128], full)
        s_ref[lo + STEP : 128, :] -= upd[lo + STEP :, :]


def factor_block(k, a_s, s_ref, e_s, u_s, inv_s, low_s, between):
    lo, hi = BLOCK * k, BLOCK * (k + 1)
    ri = lax.broadcasted_iota(jnp.int32, (BLOCK, BLOCK), 0)
    ci = lax.broadcasted_iota(jnp.int32, (BLOCK, BLOCK), 1)
    s_ref[:, 0:BLOCK] = a_s[lo:hi, lo:hi]
    s_ref[:, BLOCK:] = (ri == ci).astype(F32)
    for b in range(4):
        factor_step(s_ref, b, between)
    inverse = s_ref[:, BLOCK:]
    inv_s[k] = inverse
    if hi < PANEL:
        rest = dot(inverse, a_s[lo:hi, hi:], NN, HI)
        u_s[lo:hi, hi:] = rest
        a_s[hi : hi + BLOCK, hi:] -= dot(rest[:, 0:BLOCK], rest, TN, HI)
        if hi + BLOCK < PANEL:
            far = rest[:, BLOCK:]
            a_s[hi + BLOCK :, hi + BLOCK :] -= dot(far, far, TN, HI)
    if k % 2:
        low_s[k // 2] = dot(inverse, e_s[...], NN, HI)
    else:
        e_s[...] = -dot(rest[:, 0:BLOCK], inverse, TN, HI)


def stacked(c, modes):
    n = c.shape[1]
    high, low = split(c)
    gap = lax.broadcasted_iota(jnp.int32, (SLOTS - modes, n), 0)
    ones = (gap == 0).astype(F32).astype(BF16)
    none = jnp.zeros((SLOTS - modes, n), BF16)
    return jnp.concatenate([high, ones, low, none], axis=0)


def picked(left, right, cs):
    return split(dot(left, cs, NN) * dot(right, cs, NN))


def block_parts(t, c_s, fh, fl, lr, rr, lc, rc, gr, gc, gt, modes):
    env = {}

    def part0():
        cs = stacked(c_s[t], modes)
        env["fr"] = picked(lr[...], rr[...], cs)
        env["fc"] = picked(lc[...], rc[...], cs)
        env["fp"] = (fh[t], fl[t])

    def part1():
        gr[...] += dot3(env["fr"], env["fp"])

    def part2(at):
        gc[at, :] += dot3(tuple(half[at] for half in env["fc"]), env["fp"])

    def part3():
        gt[...] += dot3(env["fr"], env["fc"])

    mid = gc.shape[0] // 2
    lower, upper = slice(0, mid), slice(mid, 2 * mid)
    return [part0, part1, lambda: part2(lower), part3, lambda: part2(upper)]


def pair_inverse(p, inv_s, low_s):
    zero = jnp.zeros((BLOCK, BLOCK), F32)
    top = jnp.concatenate([inv_s[2 * p], zero], 1)
    return jnp.concatenate([top, jnp.concatenate([low_s[p], inv_s[2 * p + 1]], 1)], 0)


def diagonal(shape, first_row, first_col, values):
    ri = first_row + lax.broadcasted_iota(jnp.int32, shape, 0)
    ci = first_col + lax.broadcasted_iota(jnp.int32, shape, 1)
    return jnp.where(ri == ci, values, 0.0)


def diagonal(shape, first_row, first_col, values):
    ri = first_row + lax.broadcasted_iota(jnp.int32, shape, 0)
    ci = first_col + lax.broadcasted_iota(jnp.int32, shape, 1)
    return jnp.where(ri == ci, values, 0.0)


def early_kernel(modes, scale, first, *refs):
    own, oth, lr, rr, lc, rc = refs[0:6]
    if first:
        scal, ridge_panel, ridge_cols = refs[6:9]
        a_out, gr, gc, gt, c_s, f_s, fh, fl, a_s, pair_s = refs[9:]
        pair_s[...] = jnp.zeros_like(pair_s)
        gc[...] = diagonal(gc.shape, scal[1], 0, ridge_panel[...])
        gt[...] = diagonal(gt.shape, scal[0], scal[1], ridge_cols[...])
    else:
        left, gr_in, gc_in, gt_in = refs[6:10]
        a_out, gr, gr_oth, gc, gt, c_s, f_s, fh, fl, a_s, pair_s = refs[10:]
        gc[...] = gc_in[...]
        gt[...] = gt_in[...]
        pair_s[...] = jnp.zeros_like(pair_s)
        for i in range(2):
            c_s[4 + i] = left[i]
        panel_pair(4, c_s, f_s, fh, fl, modes, scale)
    for i in range(2):
        c_s[i] = own[i]
        c_s[2 + i] = oth[i]

    def corner_body(i, carry):
        panel_pair(2 * i, c_s, f_s, fh, fl, modes, scale)
        corner_pair(2 * i, fh, fl, a_s.at[i])
        return carry

    if first:
        lax.fori_loop(0, 2, corner_body, 0)
    else:
        corner_body(0, 0)
        corner_body(1, 0)
    a_out[...] = a_s[0] + a_s[1]

    def gram_body(i, carry):
        together = 1 if first else 3
        for t in range(together):
            t = together * i + t
            for part in block_parts(t, c_s, fh, fl, lr, rr, lc, rc, pair_s.at[t // 2], gc, gt, modes):
                part()
        return carry

    lax.fori_loop(0, 2, gram_body, 0)
    if first:
        gr[...] = pair_s[0]
    else:
        gr[...] = gr_in[...] + pair_s[0]
        gr_oth[...] = pair_s[2] + pair_s[1]


def early(own, oth, tables, rest, first, modes, scale, cost):
    lr, rr, lc, rc = tables
    row_pad, col_pad = lr.shape[0], lc.shape[0]
    n = own.shape[2]
    vmem = pl.BlockSpec(memory_space=pltpu.VMEM)
    smem = pl.BlockSpec(memory_space=pltpu.SMEM)
    held = 4 if first else 6
    scratch = [
        pltpu.VMEM((held, modes, n), F32),
        pltpu.VMEM((2, PANEL, n), F32),
        pltpu.VMEM((held, PANEL, n), BF16),
        pltpu.VMEM((held, PANEL, n), BF16),
        pltpu.VMEM((2, PANEL, PANEL), F32),
        pltpu.VMEM((1 if first else 3, row_pad, PANEL), F32),
    ]
    shapes = [(PANEL, PANEL)] + [(row_pad, PANEL)] * (1 if first else 2) + [(col_pad, PANEL), (row_pad, col_pad)]
    return pl.pallas_call(
        functools.partial(early_kernel, modes, scale, first),
        in_specs=[vmem] * 6 + ([smem, vmem, vmem] if first else [vmem] * 4),
        out_specs=[vmem] * len(shapes),
        out_shape=[jax.ShapeDtypeStruct(s, F32) for s in shapes],
        scratch_shapes=scratch,
        compiler_params=pltpu.CompilerParams(vmem_limit_bytes=32 * 2**20),
        cost_estimate=pl.CostEstimate(flops=cost, bytes_accessed=2**22, transcendentals=0),
        name="early_first" if first else "early_second",
    )(own, oth, lr, rr, lc, rc, *rest)


def corner_kernel(modes, scale, c_ref, a_out, fh, fl, f_s):
    for i in range(2):
        panel_pair(2 * i, c_ref, f_s, fh, fl, modes, scale)
        corner_pair(2 * i, fh, fl, a_out.at[i])


def corner_of(own, modes, scale):
    n = own.shape[2]
    vmem = pl.BlockSpec(memory_space=pltpu.VMEM)
    return pl.pallas_call(
        functools.partial(corner_kernel, modes, scale),
        in_specs=[vmem],
        out_specs=[vmem] * 3,
        out_shape=[
            jax.ShapeDtypeStruct((2, PANEL, PANEL), F32),
            jax.ShapeDtypeStruct((4, PANEL, n), BF16),
            jax.ShapeDtypeStruct((4, PANEL, n), BF16),
        ],
        scratch_shapes=[pltpu.VMEM((2, PANEL, n), F32)],
        compiler_params=pltpu.CompilerParams(vmem_limit_bytes=24 * 2**20),
        cost_estimate=pl.CostEstimate(flops=10**9, bytes_accessed=2**22, transcendentals=0),
        name="late_corner",
    )(own)


def halves_kernel(core_ref, part, offset, keep, send):
    core = core_ref[0]
    half = keep.shape[1]
    mine = pl.multiple_of(core * half, half)
    other = pl.multiple_of((1 - core) * half, half)
    send[...] = (part[pl.ds(other, half), :] - offset[...]).T
    keep[...] = (part[pl.ds(mine, half), :] - offset[...]).T


def halves(core, part, offset):
    vmem = pl.BlockSpec(memory_space=pltpu.VMEM)
    snaps, modes = part.shape
    return pl.pallas_call(
        halves_kernel,
        in_specs=[pl.BlockSpec(memory_space=pltpu.SMEM)] + [vmem] * 2,
        out_specs=[vmem] * 2,
        out_shape=[jax.ShapeDtypeStruct((modes, snaps // 2), F32)] * 2,
        compiler_params=pltpu.CompilerParams(vmem_limit_bytes=16 * 2**20),
        name="halves",
    )(core, part, offset)


LATE = 8


def main_kernel(modes, scale, scal, own, oth, lr, rr, lc, rc, ridge_panel,
                own_h, own_l, a_own, a0, a1, gr_in, gr_oth_in, gc_in, gt_in,
                tile_out, rows_out,
                f_s, fh, fl, a_p, a_s, s_s, e_s, u_s, inv_s, low_s, gr, gc, gt, pr, pc):
    first_row, first_col = scal[0], scal[1]
    rows, cols = tile_out.shape

    def corner_body(i, carry):
        panel_pair(2 * i, oth, f_s, fh, fl, modes, scale)
        a_p[i] = corner_part(2 * i, fh, fl, 0)
        return carry

    lax.fori_loop(0, 2, corner_body, 0)
    a_s[...] = diagonal(a_s.shape, 0, 0, ridge_panel[...])

    def add_corner(rows, cols, late):
        early_sum = a0[rows, cols] + a1[rows, cols]
        a_s[rows, cols] += early_sum + ((a_own[0, rows, cols] + late[0]) + (a_own[1, rows, cols] + late[1]))

    def add_low():
        half = slice(HALF, PANEL)
        add_corner(half, half, [corner_part(2 * i, fh, fl, HALF) for i in range(2)])

    add_corner(slice(0, HALF), slice(0, PANEL), a_p)
    gr[...] = jnp.zeros_like(gr)
    gc[...] = gc_in[...]
    gt[...] = gt_in[...]

    parts = []
    for t in range(LATE):
        held = (own, own_h, own_l) if t < 4 else (oth, fh, fl)
        parts += block_parts(t % 4, *held, lr, rr, lc, rc, gr.at[t // 2], gc, gt, modes)

    def solve_first(p, at, g):
        first = dot(g[:, 0:HALF], pair_inverse(0, inv_s, low_s), NT, HI)
        p[at, 0:HALF] = first
        p[at, HALF:] = g[:, HALF:] - dot(first, u_s[0:HALF, HALF:], NN, HI)

    def solve_rows():
        line = diagonal(pr.shape, first_row, 0, ridge_panel[...])
        sums = (gr_in[...] + (gr[0] + gr[1])) + (gr_oth_in[...] + (gr[2] + gr[3])) + line
        solve_first(pr, slice(0, pr.shape[0]), sums)

    def solve_cols(i):
        mid = pc.shape[0] // 2
        at = slice(mid * i, mid * i + mid)
        solve_first(pc, at, gc[at, :])

    def update(at):
        ri = first_row + lax.broadcasted_iota(jnp.int32, gt.shape, 0)
        ci = first_col + lax.broadcasted_iota(jnp.int32, gt.shape, 1)
        change = dot3(split(pr[:, at : at + HALF]), split(pc[:, at : at + HALF]))
        return gt[...] - jnp.where((ri >= PANEL) & (ci >= PANEL), change, 0.0)

    def write_rows(at):
        line = first_row + lax.broadcasted_iota(jnp.int32, (rows, HALF), 0)
        place = at + lax.broadcasted_iota(jnp.int32, (rows, HALF), 1)
        rows_out[:, at : at + HALF] = jnp.where(place <= line, pr[0:rows, at : at + HALF], 0.0)

    def update_first():
        gt[...] = update(0)
        write_rows(0)

    slots = [[] for _ in range(64)]
    for i, part in enumerate(parts):
        slots[i * 50 // len(parts)].append(part)
    slots[20].append(add_low)
    slots[51].append(solve_rows)
    slots[53].append(lambda: solve_cols(0))
    slots[55].append(lambda: solve_cols(1))
    slots[58].append(update_first)

    def between_of(k):
        def between(i):
            for part in slots[16 * k + i]:
                part()

        return between

    for k in range(4):
        factor_block(k, a_s, s_s, e_s, u_s, inv_s, low_s, between_of(k))

    inverse = pair_inverse(1, inv_s, low_s)
    for p in (pr, pc):
        p[:, HALF:] = dot(p[:, HALF:], inverse, NT, HI)
    tile_out[...] = update(HALF)[0:rows, 0:cols]
    write_rows(HALF)


def main(scal, own, oth, tables, ridge_panel, sums, rows, cols, scale):
    modes, n = own.shape[1:]
    lr, rr, lc, rc = tables
    row_pad, col_pad = lr.shape[0], lc.shape[0]
    vmem = pl.BlockSpec(memory_space=pltpu.VMEM)
    return pl.pallas_call(
        functools.partial(main_kernel, modes, scale),
        in_specs=[pl.BlockSpec(memory_space=pltpu.SMEM)] + [vmem] * 16,
        out_specs=[vmem, vmem],
        out_shape=[jax.ShapeDtypeStruct((rows, cols), F32), jax.ShapeDtypeStruct((rows, PANEL), F32)],
        scratch_shapes=[
            pltpu.VMEM((2, PANEL, n), F32),
            pltpu.VMEM((4, PANEL, n), BF16),
            pltpu.VMEM((4, PANEL, n), BF16),
            pltpu.VMEM((2, HALF, PANEL), F32),
            pltpu.VMEM((PANEL, PANEL), F32),
            pltpu.VMEM((BLOCK, 2 * BLOCK), F32),
            pltpu.VMEM((BLOCK, BLOCK), F32),
            pltpu.VMEM((PANEL, PANEL), F32),
            pltpu.VMEM((4, BLOCK, BLOCK), F32),
            pltpu.VMEM((2, BLOCK, BLOCK), F32),
            pltpu.VMEM((LATE // 2, row_pad, PANEL), F32),
            pltpu.VMEM((col_pad, PANEL), F32),
            pltpu.VMEM((row_pad, col_pad), F32),
            pltpu.VMEM((row_pad, PANEL), F32),
            pltpu.VMEM((col_pad, PANEL), F32),
        ],
        compiler_params=pltpu.CompilerParams(vmem_limit_bytes=32 * 2**20),
        name="gram_factor",
    )(scal, own, oth, lr, rr, lc, rc, ridge_panel, *sums)


def swap(value, axis, bit, other_bit=None):
    size = lax.axis_size(axis)
    bits = (bit, bit if other_bit is None else other_bit)
    return lax.ppermute(value, axis, [(i, i ^ bits[i & 1]) for i in range(size)])


def padded(count):
    return -(-count // 16) * 16


def per_device(snapshots, pod_basis, reference_field, ridge_weights):
    modes = pod_basis.shape[0]
    snap_total = snapshots.shape[0] * lax.axis_size("snap")
    scale = snap_total**-0.5
    feature_total = ridge_weights.shape[0]
    rows = feature_total // lax.axis_size("cells")
    cols = feature_total // lax.axis_size("snap")
    group = lax.axis_index("snap")
    core = lax.axis_index("cells") & 1
    first_row = lax.axis_index("cells") * rows
    first_col = group * cols
    scal = jnp.stack([first_row, first_col]).astype(jnp.int32)
    tables = picks(scal, padded(rows), padded(cols), modes, scale)
    ridge_panel = ridge_weights[None, :PANEL]
    ridge_cols = lax.dynamic_slice_in_dim(ridge_weights, first_col, cols)
    ridge_cols = jnp.pad(ridge_cols, (0, padded(cols) - cols))[None, :]

    projected = lax.dot_general(snapshots, pod_basis, NT, preferred_element_type=F32)
    offset = lax.dot_general(reference_field[None, :], pod_basis, NT, preferred_element_type=F32)
    keep, send = halves(core[None].astype(jnp.int32), projected, offset)
    total = keep + swap(send, "cells", 1)
    for bit, other_bit in ((2, 4), (4, 2), (8, 8)):
        total = total + swap(total, "cells", bit, other_bit)

    together = lax.optimization_barrier
    own0 = total[None]
    own1 = swap(own0, "snap", 4)
    oth0 = swap(own0, "cells", 1)
    own1, oth0, tables, ridge_panel, ridge_cols = together((own1, oth0, tables, ridge_panel, ridge_cols))
    pair = jnp.concatenate([own0, own1], 0)
    own2 = swap(pair, "snap", 2)
    oth_pair = jnp.concatenate([oth0, swap(own1, "cells", 1)], 0)
    sums = early(pair, oth_pair, tables, (scal, ridge_panel, ridge_cols), True, modes, scale, 4 * 10**9)
    own2, a0, *sums = together((own2, *sums))
    own3 = swap(jnp.concatenate([pair, own2], 0), "snap", 1)
    oth2 = swap(own2, "cells", 1)
    sums = early(own2, oth2, tables, (oth_pair, *sums), False, modes, scale, 4 * 10**9)
    own3, a1, *sums = together((own3, *sums))
    oth3 = swap(own3, "cells", 1)
    a_own, own_h, own_l = corner_of(own3, modes, scale)
    oth3, a_own, own_h, own_l = together((oth3, a_own, own_h, own_l))
    given = (own_h, own_l, a_own, a0, a1, *sums)
    return tuple(main(scal, own3, oth3, tables, ridge_panel, given, rows, cols, scale))


def solution(mesh):
    return jax.shard_map(
        per_device,
        mesh=mesh,
        in_specs=(P("snap", "cells"), P(None, "cells"), P("cells"), P()),
        out_specs=(P("cells", "snap"), P("cells", None)),
        check_vma=False,
    )
```

```python
import functools
import math

import jax
import jax.numpy as jnp
import numpy as np
from jax import lax
from jax.experimental import pallas as pl
from jax.experimental.pallas import tpu as pltpu
from jax.sharding import PartitionSpec as P

PANEL = 512
HI = lax.Precision.HIGHEST
HALF = 256
BLOCK = 128
STEP = 32
SLOTS = 112
F32 = jnp.float32
BF16 = jnp.bfloat16
NT = (((1,), (1,)), ((), ()))
TN = (((0,), (0,)), ((), ()))
NN = (((1,), (0,)), ((), ()))


def dot(a, b, dims, precision=None):
    return lax.dot_general(a, b, dims, precision=precision, preferred_element_type=F32)


def split(value):
    high = value.astype(BF16)
    return high, (value - high.astype(F32)).astype(BF16)


def dot3(a, b):
    ah, al = a
    bh, bl = b
    return dot(jnp.concatenate([ah, ah, al], 1), jnp.concatenate([bh, bl, bh], 1), NT)


def pick_tables(first, rows, modes):
    index = first + lax.broadcasted_iota(jnp.int32, (rows, 128), 0)
    slot = lax.broadcasted_iota(jnp.int32, (rows, 128), 1)

    def offset(a):
        return modes + modes * a - (a * (a - 1)) // 2

    linear = index < modes
    here = (index >= offset(slot)) & (index < offset(slot + 1)) & (slot < modes)
    right_value = jnp.where(here, index - offset(slot) + slot, 0).astype(F32)
    right_index = jnp.sum(right_value, axis=1, keepdims=True).astype(jnp.int32)
    left_index = jnp.sum(jnp.where(here, slot, 0).astype(F32), axis=1, keepdims=True).astype(jnp.int32)
    left_index = jnp.where(linear, index, left_index)
    right_index = jnp.where(linear, modes, right_index)
    return (slot == left_index).astype(F32), (slot == right_index).astype(F32)


def pick_kernel(modes, scale, scal, lr, rr, lc, rc):
    for ref_l, ref_r, first in ((lr, rr, scal[0]), (lc, rc, scal[1])):
        block = math.gcd(lr.shape[0], ref_l.shape[0])

        def rows_body(i, carry, ref_l=ref_l, ref_r=ref_r, first=first):
            at = pl.ds(pl.multiple_of(i * block, 16), block)
            left, right = pick_tables(first + i * block, block, modes)
            for ref, value in ((ref_l, left * scale), (ref_r, right)):
                ref[at, 0:SLOTS] = value[:, 0:SLOTS].astype(BF16)
                ref[at, SLOTS : 2 * SLOTS] = value[:, 0:SLOTS].astype(BF16)
            return carry

        lax.fori_loop(0, ref_l.shape[0] // block, rows_body, 0)


def picks(scal, row_pad, col_pad, modes, scale):
    shapes = [(row_pad, 2 * SLOTS)] * 2 + [(col_pad, 2 * SLOTS)] * 2
    return pl.pallas_call(
        functools.partial(pick_kernel, modes, scale),
        in_specs=[pl.BlockSpec(memory_space=pltpu.SMEM)],
        out_shape=[jax.ShapeDtypeStruct(s, BF16) for s in shapes],
        compiler_params=pltpu.CompilerParams(vmem_limit_bytes=40 * 2**20),
        name="picks",
    )(scal)


def panel_features(c_ref, t, f_ref, modes, scale):
    f_ref[0:modes, :] = c_ref[t] * scale
    at, a = modes, 0
    while at < PANEL:
        count = min(modes - a, PANEL - at)
        f_ref[at : at + count, :] = c_ref[t, a : a + count, :] * (c_ref[t, a : a + 1, :] * scale)
        at += count
        a += 1


def panel_pair(t, c_s, f_s, fh, fl, modes, scale):
    for i in range(2):
        panel_features(c_s, t + i, f_s.at[i], modes, scale)
        fh[t + i], fl[t + i] = split(f_s[i])


def corner_part(t, fh, fl, at):
    def one(i):
        h, l = fh[t + i], fl[t + i]
        rows = slice(at, at + HALF)
        return dot3((h[rows], l[rows]), (h[at:], l[at:]))

    return one(0) + one(1)


def corner_pair(t, fh, fl, a_ref):
    a_ref[0:HALF, :] = corner_part(t, fh, fl, 0)
    a_ref[HALF:, HALF:] = corner_part(t, fh, fl, HALF)


def lane_bcast(x, c):
    return jnp.broadcast_to(x[:, c : c + 1], (8, 128))


def sub_bcast(x, k):
    return jnp.broadcast_to(x[k : k + 1, :], (8, 128))


def split3(value):
    high = value.astype(BF16)
    rest = value - high.astype(F32)
    middle = rest.astype(BF16)
    return high, middle, (rest - middle.astype(F32)).astype(BF16)


def update_dot(left, right):
    lh, lm, ll = split3(left)
    rh, rm, rl = split3(right)
    return dot(
        jnp.concatenate([lh, lh, lh, lm, lm, ll], 0), jnp.concatenate([rh, rm, rl, rh, rm, rh], 0), TN
    )


def factor_step(s_ref, b, between):
    lo = STEP * b
    strips = STEP // 8
    sub = lax.broadcasted_iota(jnp.int32, (8, 128), 0)
    T = [[s_ref[lo + 8 * r : lo + 8 * r + 8, 0:128], s_ref[lo + 8 * r : lo + 8 * r + 8, 128:256]] for r in range(strips)]
    for q in range(strips):
        cols = range(8 * q, 8 * q + 8)
        B = {(r, j): lane_bcast(T[r][0], lo + j) for j in cols for r in range(q, strips)}
        scale = None
        for k in cols:
            rs = lax.rsqrt(sub_bcast(B[q, k], k - 8 * q))
            inv = rs * rs
            scale = rs if scale is None else jnp.where(sub == k - 8 * q, rs, scale)
            row = [sub_bcast(part, k - 8 * q) for part in T[q]]
            pivots = {j: sub_bcast(B[q, k], j - 8 * q) for j in range(k + 1, 8 * q + 8)}
            for r in range(q, strips):
                m = B[r, k] * inv
                if r == q:
                    m = jnp.where(sub > k - 8 * q, m, 0.0)
                for j in pivots:
                    B[r, j] = B[r, j] - m * pivots[j]
                T[r] = [part - m * line for part, line in zip(T[r], row)]
        T[q] = [part * scale for part in T[q]]
        between(4 * b + q)
    for r in range(strips):
        s_ref[lo + 8 * r : lo + 8 * r + 8, 0:128] = T[r][0]
        s_ref[lo + 8 * r : lo + 8 * r + 8, 128:256] = T[r][1]
    if b < 3:
        full = s_ref[lo : lo + STEP, :]
        upd = update_dot(full[:, 0:128], full)
        s_ref[lo + STEP : 128, :] -= upd[lo + STEP :, :]


def factor_block(k, a_s, s_ref, e_s, u_s, inv_s, low_s, between):
    lo, hi = BLOCK * k, BLOCK * (k + 1)
    ri = lax.broadcasted_iota(jnp.int32, (BLOCK, BLOCK), 0)
    ci = lax.broadcasted_iota(jnp.int32, (BLOCK, BLOCK), 1)
    s_ref[:, 0:BLOCK] = a_s[lo:hi, lo:hi]
    s_ref[:, BLOCK:] = (ri == ci).astype(F32)
    for b in range(4):
        factor_step(s_ref, b, between)
    inverse = s_ref[:, BLOCK:]
    inv_s[k] = inverse
    if hi < PANEL:
        rest = dot(inverse, a_s[lo:hi, hi:], NN, HI)
        u_s[lo:hi, hi:] = rest
        a_s[hi : hi + BLOCK, hi:] -= dot(rest[:, 0:BLOCK], rest, TN, HI)
        if hi + BLOCK < PANEL:
            far = rest[:, BLOCK:]
            a_s[hi + BLOCK :, hi + BLOCK :] -= dot(far, far, TN, HI)
    if k % 2:
        low_s[k // 2] = dot(inverse, e_s[...], NN, HI)
    else:
        e_s[...] = -dot(rest[:, 0:BLOCK], inverse, TN, HI)


def stacked(c, modes):
    n = c.shape[1]
    high, low = split(c)
    gap = lax.broadcasted_iota(jnp.int32, (SLOTS - modes, n), 0)
    ones = (gap == 0).astype(F32).astype(BF16)
    none = jnp.zeros((SLOTS - modes, n), BF16)
    return jnp.concatenate([high, ones, low, none], axis=0)


def picked(left, right, cs):
    return split(dot(left, cs, NN) * dot(right, cs, NN))


def block_parts(t, c_s, fh, fl, lr, rr, lc, rc, gr, gc, gt, modes, start=None):
    env = {}
    gr_was, gc_was, gt_was = start or (gr, gc, gt)

    def part0():
        cs = stacked(c_s[t], modes)
        env["fr"] = picked(lr[...], rr[...], cs)
        env["fc"] = picked(lc[...], rc[...], cs)
        env["fp"] = (fh[t], fl[t])

    def part1():
        value = dot3(env["fr"], env["fp"])
        gr[...] = value if gr_was is None else gr_was[...] + value

    def part2(at):
        gc[at, :] = gc_was[at, :] + dot3(tuple(half[at] for half in env["fc"]), env["fp"])

    def part3():
        gt[...] = gt_was[...] + dot3(env["fr"], env["fc"])

    mid = gc.shape[0] // 2
    lower, upper = slice(0, mid), slice(mid, 2 * mid)
    return [part0, part1, lambda: part2(lower), part3, lambda: part2(upper)]


def pair_inverse(p, inv_s, low_s):
    zero = jnp.zeros((BLOCK, BLOCK), F32)
    top = jnp.concatenate([inv_s[2 * p], zero], 1)
    return jnp.concatenate([top, jnp.concatenate([low_s[p], inv_s[2 * p + 1]], 1)], 0)


def diagonal(shape, first_row, first_col, values):
    ri = first_row + lax.broadcasted_iota(jnp.int32, shape, 0)
    ci = first_col + lax.broadcasted_iota(jnp.int32, shape, 1)
    return jnp.where(ri == ci, values, 0.0)


def diagonal(shape, first_row, first_col, values):
    ri = first_row + lax.broadcasted_iota(jnp.int32, shape, 0)
    ci = first_col + lax.broadcasted_iota(jnp.int32, shape, 1)
    return jnp.where(ri == ci, values, 0.0)


def early_kernel(modes, scale, first, *refs):
    own, oth, lr, rr, lc, rc = refs[0:6]
    if first:
        scal, ridge_panel, ridge_cols = refs[6:9]
        a_out, gr, gc, gt, c_s, f_s, fh, fl, a_s, pair_s = refs[9:]
        pair_s[...] = jnp.zeros_like(pair_s)
        gc[...] = diagonal(gc.shape, scal[1], 0, ridge_panel[...])
        gt[...] = diagonal(gt.shape, scal[0], scal[1], ridge_cols[...])
    else:
        left, gr_in, gc_in, gt_in = refs[6:10]
        a_out, gr, gr_oth, gc, gt, c_s, f_s, fh, fl, a_s, pair_s = refs[10:]
        gc[...] = gc_in[...]
        gt[...] = gt_in[...]
        pair_s[...] = jnp.zeros_like(pair_s)
        for i in range(2):
            c_s[4 + i] = left[i]
        panel_pair(4, c_s, f_s, fh, fl, modes, scale)
    for i in range(2):
        c_s[i] = own[i]
        c_s[2 + i] = oth[i]

    def corner_body(i, carry):
        panel_pair(2 * i, c_s, f_s, fh, fl, modes, scale)
        corner_pair(2 * i, fh, fl, a_s.at[i])
        return carry

    if first:
        lax.fori_loop(0, 2, corner_body, 0)
    else:
        corner_body(0, 0)
        corner_body(1, 0)
    a_out[...] = a_s[0] + a_s[1]

    def gram_body(i, carry):
        together = 1 if first else 3
        for t in range(together):
            t = together * i + t
            for part in block_parts(t, c_s, fh, fl, lr, rr, lc, rc, pair_s.at[t // 2], gc, gt, modes):
                part()
        return carry

    lax.fori_loop(0, 2, gram_body, 0)
    if first:
        gr[...] = pair_s[0]
    else:
        gr[...] = gr_in[...] + pair_s[0]
        gr_oth[...] = pair_s[2] + pair_s[1]


def early(own, oth, tables, rest, first, modes, scale, cost):
    lr, rr, lc, rc = tables
    row_pad, col_pad = lr.shape[0], lc.shape[0]
    n = own.shape[2]
    vmem = pl.BlockSpec(memory_space=pltpu.VMEM)
    smem = pl.BlockSpec(memory_space=pltpu.SMEM)
    held = 4 if first else 6
    scratch = [
        pltpu.VMEM((held, modes, n), F32),
        pltpu.VMEM((2, PANEL, n), F32),
        pltpu.VMEM((held, PANEL, n), BF16),
        pltpu.VMEM((held, PANEL, n), BF16),
        pltpu.VMEM((2, PANEL, PANEL), F32),
        pltpu.VMEM((1 if first else 3, row_pad, PANEL), F32),
    ]
    shapes = [(PANEL, PANEL)] + [(row_pad, PANEL)] * (1 if first else 2) + [(col_pad, PANEL), (row_pad, col_pad)]
    return pl.pallas_call(
        functools.partial(early_kernel, modes, scale, first),
        in_specs=[vmem] * 6 + ([smem, vmem, vmem] if first else [vmem] * 4),
        out_specs=[vmem] * len(shapes),
        out_shape=[jax.ShapeDtypeStruct(s, F32) for s in shapes],
        scratch_shapes=scratch,
        compiler_params=pltpu.CompilerParams(vmem_limit_bytes=32 * 2**20),
        cost_estimate=pl.CostEstimate(flops=cost, bytes_accessed=2**22, transcendentals=0),
        name="early_first" if first else "early_second",
    )(own, oth, lr, rr, lc, rc, *rest)


def corner_kernel(modes, scale, c_ref, a_out, fh, fl, f_s):
    for i in range(2):
        panel_pair(2 * i, c_ref, f_s, fh, fl, modes, scale)
        corner_pair(2 * i, fh, fl, a_out.at[i])


def corner_of(own, modes, scale):
    n = own.shape[2]
    vmem = pl.BlockSpec(memory_space=pltpu.VMEM)
    return pl.pallas_call(
        functools.partial(corner_kernel, modes, scale),
        in_specs=[vmem],
        out_specs=[vmem] * 3,
        out_shape=[
            jax.ShapeDtypeStruct((2, PANEL, PANEL), F32),
            jax.ShapeDtypeStruct((4, PANEL, n), BF16),
            jax.ShapeDtypeStruct((4, PANEL, n), BF16),
        ],
        scratch_shapes=[pltpu.VMEM((2, PANEL, n), F32)],
        compiler_params=pltpu.CompilerParams(vmem_limit_bytes=24 * 2**20),
        cost_estimate=pl.CostEstimate(flops=10**9, bytes_accessed=2**22, transcendentals=0),
        name="late_corner",
    )(own)


def halves_kernel(core_ref, part, offset, keep, send):
    core = core_ref[0]
    half = keep.shape[1]
    mine = pl.multiple_of(core * half, half)
    other = pl.multiple_of((1 - core) * half, half)
    send[...] = (part[pl.ds(other, half), :] - offset[...]).T
    keep[...] = (part[pl.ds(mine, half), :] - offset[...]).T


def halves(core, part, offset):
    vmem = pl.BlockSpec(memory_space=pltpu.VMEM)
    snaps, modes = part.shape
    return pl.pallas_call(
        halves_kernel,
        in_specs=[pl.BlockSpec(memory_space=pltpu.SMEM)] + [vmem] * 2,
        out_specs=[vmem] * 2,
        out_shape=[jax.ShapeDtypeStruct((modes, snaps // 2), F32)] * 2,
        compiler_params=pltpu.CompilerParams(vmem_limit_bytes=16 * 2**20),
        name="halves",
    )(core, part, offset)


LATE = 8


def main_kernel(modes, scale, scal, own, oth, lr, rr, lc, rc, ridge_panel,
                own_h, own_l, a_own, a0, a1, gr_in, gr_oth_in, gc_in, gt_in,
                tile_out, rows_out,
                f_s, fh, fl, a_p, a_s, s_s, e_s, u_s, inv_s, low_s, gr, gc, gt, pr, pc):
    first_row, first_col = scal[0], scal[1]
    rows, cols = tile_out.shape

    def corner_body(i, carry):
        panel_pair(2 * i, oth, f_s, fh, fl, modes, scale)
        a_p[i] = corner_part(2 * i, fh, fl, 0)
        return carry

    lax.fori_loop(0, 2, corner_body, 0)
    a_s[...] = diagonal(a_s.shape, 0, 0, ridge_panel[...])

    def add_corner(rows, cols, late):
        early_sum = a0[rows, cols] + a1[rows, cols]
        a_s[rows, cols] += early_sum + ((a_own[0, rows, cols] + late[0]) + (a_own[1, rows, cols] + late[1]))

    def add_low():
        half = slice(HALF, PANEL)
        add_corner(half, half, [corner_part(2 * i, fh, fl, HALF) for i in range(2)])

    add_corner(slice(0, HALF), slice(0, PANEL), a_p)

    parts = []
    for t in range(LATE):
        held = (own, own_h, own_l) if t < 4 else (oth, fh, fl)
        pair = gr.at[t // 2]
        start = (pair if t % 2 else None, gc if t else gc_in, gt if t else gt_in)
        parts += block_parts(t % 4, *held, lr, rr, lc, rc, pair, gc, gt, modes, start)

    def solve_first(p, at, g):
        first = dot(g[:, 0:HALF], pair_inverse(0, inv_s, low_s), NT, HI)
        p[at, 0:HALF] = first
        p[at, HALF:] = g[:, HALF:] - dot(first, u_s[0:HALF, HALF:], NN, HI)

    def solve_rows():
        line = diagonal(pr.shape, first_row, 0, ridge_panel[...])
        sums = (gr_in[...] + (gr[0] + gr[1])) + (gr_oth_in[...] + (gr[2] + gr[3])) + line
        solve_first(pr, slice(0, pr.shape[0]), sums)

    def solve_cols(i):
        mid = pc.shape[0] // 2
        at = slice(mid * i, mid * i + mid)
        solve_first(pc, at, gc[at, :])

    def update(at):
        ri = first_row + lax.broadcasted_iota(jnp.int32, gt.shape, 0)
        ci = first_col + lax.broadcasted_iota(jnp.int32, gt.shape, 1)
        change = dot3(split(pr[:, at : at + HALF]), split(pc[:, at : at + HALF]))
        return gt[...] - jnp.where((ri >= PANEL) & (ci >= PANEL), change, 0.0)

    def write_rows(at):
        line = first_row + lax.broadcasted_iota(jnp.int32, (rows, HALF), 0)
        place = at + lax.broadcasted_iota(jnp.int32, (rows, HALF), 1)
        rows_out[:, at : at + HALF] = jnp.where(place <= line, pr[0:rows, at : at + HALF], 0.0)

    def update_first():
        gt[...] = update(0)
        write_rows(0)

    slots = [[] for _ in range(64)]
    for i, part in enumerate(parts):
        slots[i * 50 // len(parts)].append(part)
    slots[20].append(add_low)
    slots[51].append(solve_rows)
    slots[53].append(lambda: solve_cols(0))
    slots[55].append(lambda: solve_cols(1))
    slots[58].append(update_first)

    def between_of(k):
        def between(i):
            for part in slots[16 * k + i]:
                part()

        return between

    for k in range(4):
        factor_block(k, a_s, s_s, e_s, u_s, inv_s, low_s, between_of(k))

    inverse = pair_inverse(1, inv_s, low_s)
    for p in (pr, pc):
        p[:, HALF:] = dot(p[:, HALF:], inverse, NT, HI)
    tile_out[...] = update(HALF)[0:rows, 0:cols]
    write_rows(HALF)


def main(scal, own, oth, tables, ridge_panel, sums, rows, cols, scale):
    modes, n = own.shape[1:]
    lr, rr, lc, rc = tables
    row_pad, col_pad = lr.shape[0], lc.shape[0]
    vmem = pl.BlockSpec(memory_space=pltpu.VMEM)
    return pl.pallas_call(
        functools.partial(main_kernel, modes, scale),
        in_specs=[pl.BlockSpec(memory_space=pltpu.SMEM)] + [vmem] * 16,
        out_specs=[vmem, vmem],
        out_shape=[jax.ShapeDtypeStruct((rows, cols), F32), jax.ShapeDtypeStruct((rows, PANEL), F32)],
        scratch_shapes=[
            pltpu.VMEM((2, PANEL, n), F32),
            pltpu.VMEM((4, PANEL, n), BF16),
            pltpu.VMEM((4, PANEL, n), BF16),
            pltpu.VMEM((2, HALF, PANEL), F32),
            pltpu.VMEM((PANEL, PANEL), F32),
            pltpu.VMEM((BLOCK, 2 * BLOCK), F32),
            pltpu.VMEM((BLOCK, BLOCK), F32),
            pltpu.VMEM((PANEL, PANEL), F32),
            pltpu.VMEM((4, BLOCK, BLOCK), F32),
            pltpu.VMEM((2, BLOCK, BLOCK), F32),
            pltpu.VMEM((LATE // 2, row_pad, PANEL), F32),
            pltpu.VMEM((col_pad, PANEL), F32),
            pltpu.VMEM((row_pad, col_pad), F32),
            pltpu.VMEM((row_pad, PANEL), F32),
            pltpu.VMEM((col_pad, PANEL), F32),
        ],
        compiler_params=pltpu.CompilerParams(vmem_limit_bytes=32 * 2**20),
        name="gram_factor",
    )(scal, own, oth, lr, rr, lc, rc, ridge_panel, *sums)


def swap(value, axis, bit, other_bit=None):
    size = lax.axis_size(axis)
    bits = (bit, bit if other_bit is None else other_bit)
    return lax.ppermute(value, axis, [(i, i ^ bits[i & 1]) for i in range(size)])


def padded(count):
    return -(-count // 16) * 16


def per_device(snapshots, pod_basis, reference_field, ridge_weights):
    modes = pod_basis.shape[0]
    snap_total = snapshots.shape[0] * lax.axis_size("snap")
    scale = snap_total**-0.5
    feature_total = ridge_weights.shape[0]
    rows = feature_total // lax.axis_size("cells")
    cols = feature_total // lax.axis_size("snap")
    group = lax.axis_index("snap")
    core = lax.axis_index("cells") & 1
    first_row = lax.axis_index("cells") * rows
    first_col = group * cols
    scal = jnp.stack([first_row, first_col]).astype(jnp.int32)
    tables = picks(scal, padded(rows), padded(cols), modes, scale)
    ridge_panel = ridge_weights[None, :PANEL]
    ridge_cols = lax.dynamic_slice_in_dim(ridge_weights, first_col, cols)
    ridge_cols = jnp.pad(ridge_cols, (0, padded(cols) - cols))[None, :]

    projected = lax.dot_general(snapshots, pod_basis, NT, preferred_element_type=F32)
    offset = lax.dot_general(reference_field[None, :], pod_basis, NT, preferred_element_type=F32)
    keep, send = halves(core[None].astype(jnp.int32), projected, offset)
    total = keep + swap(send, "cells", 1)
    for bit, other_bit in ((2, 4), (4, 2), (8, 8)):
        total = total + swap(total, "cells", bit, other_bit)

    together = lax.optimization_barrier
    own0 = total[None]
    own1 = swap(own0, "snap", 4)
    oth0 = swap(own0, "cells", 1)
    own1, oth0, tables, ridge_panel, ridge_cols = together((own1, oth0, tables, ridge_panel, ridge_cols))
    pair = jnp.concatenate([own0, own1], 0)
    own2 = swap(pair, "snap", 2)
    oth_pair = jnp.concatenate([oth0, swap(own1, "cells", 1)], 0)
    sums = early(pair, oth_pair, tables, (scal, ridge_panel, ridge_cols), True, modes, scale, 4 * 10**9)
    own2, a0, *sums = together((own2, *sums))
    own3 = swap(jnp.concatenate([pair, own2], 0), "snap", 1)
    oth2 = swap(own2, "cells", 1)
    sums = early(own2, oth2, tables, (oth_pair, *sums), False, modes, scale, 4 * 10**9)
    own3, a1, *sums = together((own3, *sums))
    oth3 = swap(own3, "cells", 1)
    a_own, own_h, own_l = corner_of(own3, modes, scale)
    oth3, a_own, own_h, own_l = together((oth3, a_own, own_h, own_l))
    given = (own_h, own_l, a_own, a0, a1, *sums)
    return tuple(main(scal, own3, oth3, tables, ridge_panel, given, rows, cols, scale))


def solution(mesh):
    return jax.shard_map(
        per_device,
        mesh=mesh,
        in_specs=(P("snap", "cells"), P(None, "cells"), P("cells"), P()),
        out_specs=(P("cells", "snap"), P("cells", None)),
        check_vma=False,
    )
```

```python
import functools
import math

import jax
import jax.numpy as jnp
import numpy as np
from jax import lax
from jax.experimental import pallas as pl
from jax.experimental.pallas import tpu as pltpu
from jax.sharding import PartitionSpec as P

PANEL = 512
HI = lax.Precision.HIGHEST
HALF = 256
BLOCK = 128
STEP = 32
SLOTS = 112
F32 = jnp.float32
BF16 = jnp.bfloat16
NT = (((1,), (1,)), ((), ()))
TN = (((0,), (0,)), ((), ()))
NN = (((1,), (0,)), ((), ()))


def dot(a, b, dims, precision=None):
    return lax.dot_general(a, b, dims, precision=precision, preferred_element_type=F32)


def split(value):
    high = value.astype(BF16)
    return high, (value - high.astype(F32)).astype(BF16)


def dot3(a, b):
    ah, al = a
    bh, bl = b
    return dot(jnp.concatenate([ah, ah, al], 1), jnp.concatenate([bh, bl, bh], 1), NT)


def pick_tables(first, rows, modes):
    index = first + lax.broadcasted_iota(jnp.int32, (rows, 128), 0)
    slot = lax.broadcasted_iota(jnp.int32, (rows, 128), 1)

    def offset(a):
        return modes + modes * a - (a * (a - 1)) // 2

    linear = index < modes
    here = (index >= offset(slot)) & (index < offset(slot + 1)) & (slot < modes)
    right_value = jnp.where(here, index - offset(slot) + slot, 0).astype(F32)
    right_index = jnp.sum(right_value, axis=1, keepdims=True).astype(jnp.int32)
    left_index = jnp.sum(jnp.where(here, slot, 0).astype(F32), axis=1, keepdims=True).astype(jnp.int32)
    left_index = jnp.where(linear, index, left_index)
    right_index = jnp.where(linear, modes, right_index)
    return (slot == left_index).astype(F32), (slot == right_index).astype(F32)


def pick_kernel(modes, scale, scal, lr, rr, lc, rc):
    for ref_l, ref_r, first in ((lr, rr, scal[0]), (lc, rc, scal[1])):
        block = math.gcd(lr.shape[0], ref_l.shape[0])

        def rows_body(i, carry, ref_l=ref_l, ref_r=ref_r, first=first):
            at = pl.ds(pl.multiple_of(i * block, 16), block)
            left, right = pick_tables(first + i * block, block, modes)
            for ref, value in ((ref_l, left * scale), (ref_r, right)):
                ref[at, 0:SLOTS] = value[:, 0:SLOTS].astype(BF16)
                ref[at, SLOTS : 2 * SLOTS] = value[:, 0:SLOTS].astype(BF16)
            return carry

        lax.fori_loop(0, ref_l.shape[0] // block, rows_body, 0)


def picks(scal, row_pad, col_pad, modes, scale):
    shapes = [(row_pad, 2 * SLOTS)] * 2 + [(col_pad, 2 * SLOTS)] * 2
    return pl.pallas_call(
        functools.partial(pick_kernel, modes, scale),
        in_specs=[pl.BlockSpec(memory_space=pltpu.SMEM)],
        out_shape=[jax.ShapeDtypeStruct(s, BF16) for s in shapes],
        compiler_params=pltpu.CompilerParams(vmem_limit_bytes=40 * 2**20),
        name="picks",
    )(scal)


def panel_features(c_ref, t, f_ref, modes, scale):
    f_ref[0:modes, :] = c_ref[t] * scale
    at, a = modes, 0
    while at < PANEL:
        count = min(modes - a, PANEL - at)
        f_ref[at : at + count, :] = c_ref[t, a : a + count, :] * (c_ref[t, a : a + 1, :] * scale)
        at += count
        a += 1


def panel_one(t, c_s, f_ref, fh, fl, modes, scale):
    panel_features(c_s, t, f_ref, modes, scale)
    fh[t], fl[t] = split(f_ref[...])


def panel_pair(t, c_s, f_s, fh, fl, modes, scale):
    for i in range(2):
        panel_one(t + i, c_s, f_s.at[i], fh, fl, modes, scale)


def corner_one(t, fh, fl, at):
    h, l = fh[t], fl[t]
    rows = slice(at, at + HALF)
    return dot3((h[rows], l[rows]), (h[at:], l[at:]))


def corner_part(t, fh, fl, at):
    return corner_one(t, fh, fl, at) + corner_one(t + 1, fh, fl, at)


def corner_pair(t, fh, fl, a_ref):
    a_ref[0:HALF, :] = corner_part(t, fh, fl, 0)
    a_ref[HALF:, HALF:] = corner_part(t, fh, fl, HALF)


def lane_bcast(x, c):
    return jnp.broadcast_to(x[:, c : c + 1], (8, 128))


def sub_bcast(x, k):
    return jnp.broadcast_to(x[k : k + 1, :], (8, 128))


def split3(value):
    high = value.astype(BF16)
    rest = value - high.astype(F32)
    middle = rest.astype(BF16)
    return high, middle, (rest - middle.astype(F32)).astype(BF16)


def update_dot(left, right):
    lh, lm, ll = split3(left)
    rh, rm, rl = split3(right)
    return dot(
        jnp.concatenate([lh, lh, lh, lm, lm, ll], 0), jnp.concatenate([rh, rm, rl, rh, rm, rh], 0), TN
    )


def factor_step(s_ref, b, between):
    lo = STEP * b
    strips = STEP // 8
    sub = lax.broadcasted_iota(jnp.int32, (8, 128), 0)
    T = [[s_ref[lo + 8 * r : lo + 8 * r + 8, 0:128], s_ref[lo + 8 * r : lo + 8 * r + 8, 128:256]] for r in range(strips)]
    for q in range(strips):
        cols = range(8 * q, 8 * q + 8)
        B = {(r, j): lane_bcast(T[r][0], lo + j) for j in cols for r in range(q, strips)}
        scale = None
        for k in cols:
            rs = lax.rsqrt(sub_bcast(B[q, k], k - 8 * q))
            inv = rs * rs
            scale = rs if scale is None else jnp.where(sub == k - 8 * q, rs, scale)
            row = [sub_bcast(part, k - 8 * q) for part in T[q]]
            pivots = {j: sub_bcast(B[q, k], j - 8 * q) for j in range(k + 1, 8 * q + 8)}
            for r in range(q, strips):
                m = B[r, k] * inv
                if r == q:
                    m = jnp.where(sub > k - 8 * q, m, 0.0)
                for j in pivots:
                    B[r, j] = B[r, j] - m * pivots[j]
                T[r] = [part - m * line for part, line in zip(T[r], row)]
        T[q] = [part * scale for part in T[q]]
        between(4 * b + q)
    for r in range(strips):
        s_ref[lo + 8 * r : lo + 8 * r + 8, 0:128] = T[r][0]
        s_ref[lo + 8 * r : lo + 8 * r + 8, 128:256] = T[r][1]
    if b < 3:
        full = s_ref[lo : lo + STEP, :]
        upd = update_dot(full[:, 0:128], full)
        s_ref[lo + STEP : 128, :] -= upd[lo + STEP :, :]


def factor_block(k, a_s, s_ref, e_s, u_s, inv_s, low_s, between):
    lo, hi = BLOCK * k, BLOCK * (k + 1)
    ri = lax.broadcasted_iota(jnp.int32, (BLOCK, BLOCK), 0)
    ci = lax.broadcasted_iota(jnp.int32, (BLOCK, BLOCK), 1)
    s_ref[:, 0:BLOCK] = a_s[lo:hi, lo:hi]
    s_ref[:, BLOCK:] = (ri == ci).astype(F32)
    for b in range(4):
        factor_step(s_ref, b, between)
    inverse = s_ref[:, BLOCK:]
    inv_s[k] = inverse
    if hi < PANEL:
        rest = dot(inverse, a_s[lo:hi, hi:], NN, HI)
        u_s[lo:hi, hi:] = rest
        a_s[hi : hi + BLOCK, hi:] -= dot(rest[:, 0:BLOCK], rest, TN, HI)
        if hi + BLOCK < PANEL:
            far = rest[:, BLOCK:]
            a_s[hi + BLOCK :, hi + BLOCK :] -= dot(far, far, TN, HI)
    if k % 2:
        low_s[k // 2] = dot(inverse, e_s[...], NN, HI)
    else:
        e_s[...] = -dot(rest[:, 0:BLOCK], inverse, TN, HI)


def stacked(c, modes):
    n = c.shape[1]
    high, low = split(c)
    gap = lax.broadcasted_iota(jnp.int32, (SLOTS - modes, n), 0)
    ones = (gap == 0).astype(F32).astype(BF16)
    none = jnp.zeros((SLOTS - modes, n), BF16)
    return jnp.concatenate([high, ones, low, none], axis=0)


def picked(left, right, cs):
    return split(dot(left, cs, NN) * dot(right, cs, NN))


def block_parts(t, c_s, fh, fl, lr, rr, lc, rc, gr, gc, gt, modes, start=None):
    env = {}
    gr_was, gc_was, gt_was = start or (gr, gc, gt)

    def part0():
        cs = stacked(c_s[t], modes)
        env["fr"] = picked(lr[...], rr[...], cs)
        env["fc"] = picked(lc[...], rc[...], cs)
        env["fp"] = (fh[t], fl[t])

    def part1():
        value = dot3(env["fr"], env["fp"])
        gr[...] = value if gr_was is None else gr_was[...] + value

    def part2(at):
        gc[at, :] = gc_was[at, :] + dot3(tuple(half[at] for half in env["fc"]), env["fp"])

    def part3():
        gt[...] = gt_was[...] + dot3(env["fr"], env["fc"])

    mid = gc.shape[0] // 2
    lower, upper = slice(0, mid), slice(mid, 2 * mid)
    return [part0, part1, lambda: part2(lower), part3, lambda: part2(upper)]


def pair_inverse(p, inv_s, low_s):
    zero = jnp.zeros((BLOCK, BLOCK), F32)
    top = jnp.concatenate([inv_s[2 * p], zero], 1)
    return jnp.concatenate([top, jnp.concatenate([low_s[p], inv_s[2 * p + 1]], 1)], 0)


def diagonal(shape, first_row, first_col, values):
    ri = first_row + lax.broadcasted_iota(jnp.int32, shape, 0)
    ci = first_col + lax.broadcasted_iota(jnp.int32, shape, 1)
    return jnp.where(ri == ci, values, 0.0)


def diagonal(shape, first_row, first_col, values):
    ri = first_row + lax.broadcasted_iota(jnp.int32, shape, 0)
    ci = first_col + lax.broadcasted_iota(jnp.int32, shape, 1)
    return jnp.where(ri == ci, values, 0.0)


def start_kernel(modes, scale, own, lr, rr, lc, rc, scal, ridge_panel, ridge_cols, a_out, gr, gc, gt, f_s, fh, fl):
    gc[...] = diagonal(gc.shape, scal[1], 0, ridge_panel[...])
    gt[...] = diagonal(gt.shape, scal[0], scal[1], ridge_cols[...])
    panel_one(0, own, f_s, fh, fl, modes, scale)
    a_out[0:HALF, :] = corner_one(0, fh, fl, 0)
    a_out[HALF:, HALF:] = corner_one(0, fh, fl, HALF)
    for part in block_parts(0, own, fh, fl, lr, rr, lc, rc, gr, gc, gt, modes, (None, gc, gt)):
        part()


def early_kernel(modes, scale, first, *refs):
    own, oth, lr, rr, lc, rc = refs[0:6]
    if first:
        a_in, gr_in, gc_in, gt_in = refs[6:10]
        a_out, gr, gr_oth, gc, gt, c_s, f_s, fh, fl, a_s, pair_s = refs[10:]
    else:
        left, gr_in, gr_oth_in, gc_in, gt_in = refs[6:11]
        a_out, gr, gr_oth, gc, gt, c_s, f_s, fh, fl, a_s, pair_s = refs[11:]
    for i in range(2):
        c_s[i] = own[i]
        c_s[2 + i] = oth[i]

    def add(t, rows, start):
        for part in block_parts(t, c_s, fh, fl, lr, rr, lc, rc, rows, gc, gt, modes, start):
            part()

    if first:
        panel_one(1, c_s, f_s.at[0], fh, fl, modes, scale)
        panel_pair(2, c_s, f_s, fh, fl, modes, scale)
        corner_pair(2, fh, fl, a_out)
        a_out[0:HALF, :] += a_in[0:HALF, :] + corner_one(1, fh, fl, 0)
        a_out[HALF:, HALF:] += a_in[HALF:, HALF:] + corner_one(1, fh, fl, HALF)
        add(1, gr, (gr_in, gc_in, gt_in))
        add(2, gr_oth, (None, gc, gt))
        return
    for i in range(2):
        panel_pair(2 * i, c_s, f_s, fh, fl, modes, scale)
        corner_pair(2 * i, fh, fl, a_s.at[i])
    a_out[...] = a_s[0] + a_s[1]
    c_s[4] = left[1]
    panel_one(4, c_s, f_s.at[0], fh, fl, modes, scale)
    add(4, gr_oth, (gr_oth_in, gc_in, gt_in))

    def pair_body(i, carry):
        add(2 * i, pair_s.at[i], (None, gc, gt))
        add(2 * i + 1, pair_s.at[i], None)
        return carry

    lax.fori_loop(0, 2, pair_body, 0)
    gr[...] = gr_in[...] + pair_s[0]
    gr_oth[...] += pair_s[1]


def start(own, tables, scal, ridge_panel, ridge_cols, modes, scale):
    lr, rr, lc, rc = tables
    row_pad, col_pad = lr.shape[0], lc.shape[0]
    n = own.shape[2]
    vmem = pl.BlockSpec(memory_space=pltpu.VMEM)
    shapes = [(PANEL, PANEL), (row_pad, PANEL), (col_pad, PANEL), (row_pad, col_pad)]
    return pl.pallas_call(
        functools.partial(start_kernel, modes, scale),
        in_specs=[vmem] * 5 + [pl.BlockSpec(memory_space=pltpu.SMEM)] + [vmem] * 2,
        out_specs=[vmem] * 4,
        out_shape=[jax.ShapeDtypeStruct(s, F32) for s in shapes],
        scratch_shapes=[
            pltpu.VMEM((PANEL, n), F32),
            pltpu.VMEM((1, PANEL, n), BF16),
            pltpu.VMEM((1, PANEL, n), BF16),
        ],
        compiler_params=pltpu.CompilerParams(vmem_limit_bytes=24 * 2**20),
        cost_estimate=pl.CostEstimate(flops=10**9, bytes_accessed=2**22, transcendentals=0),
        name="early_start",
    )(own, lr, rr, lc, rc, scal, ridge_panel, ridge_cols)


def early(own, oth, tables, rest, first, modes, scale, cost):
    lr, rr, lc, rc = tables
    row_pad, col_pad = lr.shape[0], lc.shape[0]
    n = own.shape[2]
    vmem = pl.BlockSpec(memory_space=pltpu.VMEM)
    held = 4 if first else 5
    shapes = [(PANEL, PANEL)] + [(row_pad, PANEL)] * 2 + [(col_pad, PANEL), (row_pad, col_pad)]
    return pl.pallas_call(
        functools.partial(early_kernel, modes, scale, first),
        in_specs=[vmem] * (6 + len(rest)),
        out_specs=[vmem] * len(shapes),
        out_shape=[jax.ShapeDtypeStruct(s, F32) for s in shapes],
        scratch_shapes=[
            pltpu.VMEM((held, modes, n), F32),
            pltpu.VMEM((2, PANEL, n), F32),
            pltpu.VMEM((held, PANEL, n), BF16),
            pltpu.VMEM((held, PANEL, n), BF16),
            pltpu.VMEM((2, PANEL, PANEL), F32),
            pltpu.VMEM((2, row_pad, PANEL), F32),
        ],
        compiler_params=pltpu.CompilerParams(vmem_limit_bytes=32 * 2**20),
        cost_estimate=pl.CostEstimate(flops=cost, bytes_accessed=2**22, transcendentals=0),
        name="early_first" if first else "early_second",
    )(own, oth, lr, rr, lc, rc, *rest)


def corner_kernel(modes, scale, c_ref, a_out, fh, fl, f_s):
    for i in range(2):
        panel_pair(2 * i, c_ref, f_s, fh, fl, modes, scale)
        corner_pair(2 * i, fh, fl, a_out.at[i])


def corner_of(own, modes, scale):
    n = own.shape[2]
    vmem = pl.BlockSpec(memory_space=pltpu.VMEM)
    return pl.pallas_call(
        functools.partial(corner_kernel, modes, scale),
        in_specs=[vmem],
        out_specs=[vmem] * 3,
        out_shape=[
            jax.ShapeDtypeStruct((2, PANEL, PANEL), F32),
            jax.ShapeDtypeStruct((4, PANEL, n), BF16),
            jax.ShapeDtypeStruct((4, PANEL, n), BF16),
        ],
        scratch_shapes=[pltpu.VMEM((2, PANEL, n), F32)],
        compiler_params=pltpu.CompilerParams(vmem_limit_bytes=24 * 2**20),
        cost_estimate=pl.CostEstimate(flops=10**9, bytes_accessed=2**22, transcendentals=0),
        name="late_corner",
    )(own)


def halves_kernel(core_ref, part, offset, keep, send):
    core = core_ref[0]
    half = keep.shape[1]
    mine = pl.multiple_of(core * half, half)
    other = pl.multiple_of((1 - core) * half, half)
    send[...] = (part[pl.ds(other, half), :] - offset[...]).T
    keep[...] = (part[pl.ds(mine, half), :] - offset[...]).T


def halves(core, part, offset):
    vmem = pl.BlockSpec(memory_space=pltpu.VMEM)
    snaps, modes = part.shape
    return pl.pallas_call(
        halves_kernel,
        in_specs=[pl.BlockSpec(memory_space=pltpu.SMEM)] + [vmem] * 2,
        out_specs=[vmem] * 2,
        out_shape=[jax.ShapeDtypeStruct((modes, snaps // 2), F32)] * 2,
        compiler_params=pltpu.CompilerParams(vmem_limit_bytes=16 * 2**20),
        name="halves",
    )(core, part, offset)


LATE = 8


def main_kernel(modes, scale, scal, own, oth, lr, rr, lc, rc, ridge_panel,
                own_h, own_l, a_own, a0, a1, gr_in, gr_oth_in, gc_in, gt_in,
                tile_out, rows_out,
                f_s, fh, fl, a_p, a_s, s_s, e_s, u_s, inv_s, low_s, gr, gc, gt, pr, pc):
    first_row, first_col = scal[0], scal[1]
    rows, cols = tile_out.shape

    def corner_body(i, carry):
        panel_pair(2 * i, oth, f_s, fh, fl, modes, scale)
        a_p[i] = corner_part(2 * i, fh, fl, 0)
        return carry

    lax.fori_loop(0, 2, corner_body, 0)
    a_s[...] = diagonal(a_s.shape, 0, 0, ridge_panel[...])

    def add_corner(rows, cols, late):
        early_sum = a0[rows, cols] + a1[rows, cols]
        a_s[rows, cols] += early_sum + ((a_own[0, rows, cols] + late[0]) + (a_own[1, rows, cols] + late[1]))

    def add_low():
        half = slice(HALF, PANEL)
        add_corner(half, half, [corner_part(2 * i, fh, fl, HALF) for i in range(2)])

    add_corner(slice(0, HALF), slice(0, PANEL), a_p)

    parts = []
    for t in range(LATE):
        held = (own, own_h, own_l) if t < 4 else (oth, fh, fl)
        pair = gr.at[t // 2]
        start = (pair if t % 2 else None, gc if t else gc_in, gt if t else gt_in)
        parts += block_parts(t % 4, *held, lr, rr, lc, rc, pair, gc, gt, modes, start)

    def solve_first(p, at, g):
        first = dot(g[:, 0:HALF], pair_inverse(0, inv_s, low_s), NT, HI)
        p[at, 0:HALF] = first
        p[at, HALF:] = g[:, HALF:] - dot(first, u_s[0:HALF, HALF:], NN, HI)

    def solve_rows():
        line = diagonal(pr.shape, first_row, 0, ridge_panel[...])
        sums = (gr_in[...] + (gr[0] + gr[1])) + (gr_oth_in[...] + (gr[2] + gr[3])) + line
        solve_first(pr, slice(0, pr.shape[0]), sums)

    def solve_cols(i):
        mid = pc.shape[0] // 2
        at = slice(mid * i, mid * i + mid)
        solve_first(pc, at, gc[at, :])

    def update(at):
        ri = first_row + lax.broadcasted_iota(jnp.int32, gt.shape, 0)
        ci = first_col + lax.broadcasted_iota(jnp.int32, gt.shape, 1)
        change = dot3(split(pr[:, at : at + HALF]), split(pc[:, at : at + HALF]))
        return gt[...] - jnp.where((ri >= PANEL) & (ci >= PANEL), change, 0.0)

    def write_rows(at):
        line = first_row + lax.broadcasted_iota(jnp.int32, (rows, HALF), 0)
        place = at + lax.broadcasted_iota(jnp.int32, (rows, HALF), 1)
        rows_out[:, at : at + HALF] = jnp.where(place <= line, pr[0:rows, at : at + HALF], 0.0)

    def update_first():
        gt[...] = update(0)
        write_rows(0)

    slots = [[] for _ in range(64)]
    for i, part in enumerate(parts):
        slots[i * 50 // len(parts)].append(part)
    slots[20].append(add_low)
    slots[51].append(solve_rows)
    slots[53].append(lambda: solve_cols(0))
    slots[55].append(lambda: solve_cols(1))
    slots[58].append(update_first)

    def between_of(k):
        def between(i):
            for part in slots[16 * k + i]:
                part()

        return between

    for k in range(4):
        factor_block(k, a_s, s_s, e_s, u_s, inv_s, low_s, between_of(k))

    inverse = pair_inverse(1, inv_s, low_s)
    for p in (pr, pc):
        p[:, HALF:] = dot(p[:, HALF:], inverse, NT, HI)
    tile_out[...] = update(HALF)[0:rows, 0:cols]
    write_rows(HALF)


def main(scal, own, oth, tables, ridge_panel, sums, rows, cols, scale):
    modes, n = own.shape[1:]
    lr, rr, lc, rc = tables
    row_pad, col_pad = lr.shape[0], lc.shape[0]
    vmem = pl.BlockSpec(memory_space=pltpu.VMEM)
    return pl.pallas_call(
        functools.partial(main_kernel, modes, scale),
        in_specs=[pl.BlockSpec(memory_space=pltpu.SMEM)] + [vmem] * 16,
        out_specs=[vmem, vmem],
        out_shape=[jax.ShapeDtypeStruct((rows, cols), F32), jax.ShapeDtypeStruct((rows, PANEL), F32)],
        scratch_shapes=[
            pltpu.VMEM((2, PANEL, n), F32),
            pltpu.VMEM((4, PANEL, n), BF16),
            pltpu.VMEM((4, PANEL, n), BF16),
            pltpu.VMEM((2, HALF, PANEL), F32),
            pltpu.VMEM((PANEL, PANEL), F32),
            pltpu.VMEM((BLOCK, 2 * BLOCK), F32),
            pltpu.VMEM((BLOCK, BLOCK), F32),
            pltpu.VMEM((PANEL, PANEL), F32),
            pltpu.VMEM((4, BLOCK, BLOCK), F32),
            pltpu.VMEM((2, BLOCK, BLOCK), F32),
            pltpu.VMEM((LATE // 2, row_pad, PANEL), F32),
            pltpu.VMEM((col_pad, PANEL), F32),
            pltpu.VMEM((row_pad, col_pad), F32),
            pltpu.VMEM((row_pad, PANEL), F32),
            pltpu.VMEM((col_pad, PANEL), F32),
        ],
        compiler_params=pltpu.CompilerParams(vmem_limit_bytes=32 * 2**20),
        name="gram_factor",
    )(scal, own, oth, lr, rr, lc, rc, ridge_panel, *sums)


def swap(value, axis, bit, other_bit=None):
    size = lax.axis_size(axis)
    bits = (bit, bit if other_bit is None else other_bit)
    return lax.ppermute(value, axis, [(i, i ^ bits[i & 1]) for i in range(size)])


def padded(count):
    return -(-count // 16) * 16


def per_device(snapshots, pod_basis, reference_field, ridge_weights):
    modes = pod_basis.shape[0]
    snap_total = snapshots.shape[0] * lax.axis_size("snap")
    scale = snap_total**-0.5
    feature_total = ridge_weights.shape[0]
    rows = feature_total // lax.axis_size("cells")
    cols = feature_total // lax.axis_size("snap")
    group = lax.axis_index("snap")
    core = lax.axis_index("cells") & 1
    first_row = lax.axis_index("cells") * rows
    first_col = group * cols
    scal = jnp.stack([first_row, first_col]).astype(jnp.int32)
    tables = picks(scal, padded(rows), padded(cols), modes, scale)
    ridge_panel = ridge_weights[None, :PANEL]
    ridge_cols = lax.dynamic_slice_in_dim(ridge_weights, first_col, cols)
    ridge_cols = jnp.pad(ridge_cols, (0, padded(cols) - cols))[None, :]

    projected = lax.dot_general(snapshots, pod_basis, NT, preferred_element_type=F32)
    offset = lax.dot_general(reference_field[None, :], pod_basis, NT, preferred_element_type=F32)
    keep, send = halves(core[None].astype(jnp.int32), projected, offset)
    total = keep + swap(send, "cells", 1)
    together = lax.optimization_barrier
    for bit, other_bit in ((2, 4), (4, 2), (8, 8)):
        got = swap(total, "cells", bit, other_bit)
        if bit == 4:
            got, tables, ridge_panel, ridge_cols = together((got, tables, ridge_panel, ridge_cols))
        total = total + got

    own0 = total[None]
    own1 = swap(own0, "snap", 4)
    oth0 = swap(own0, "cells", 1)
    sums = start(own0, tables, scal, ridge_panel, ridge_cols, modes, scale)
    own1, oth0, *sums = together((own1, oth0, *sums))
    pair = jnp.concatenate([own0, own1], 0)
    own2 = swap(pair, "snap", 2)
    oth_pair = jnp.concatenate([oth0, swap(own1, "cells", 1)], 0)
    sums = early(pair, oth_pair, tables, sums, True, modes, scale, 4 * 10**9)
    own2, a0, *sums = together((own2, *sums))
    own3 = swap(jnp.concatenate([pair, own2], 0), "snap", 1)
    oth2 = swap(own2, "cells", 1)
    sums = early(own2, oth2, tables, (oth_pair, *sums), False, modes, scale, 4 * 10**9)
    own3, a1, *sums = together((own3, *sums))
    oth3 = swap(own3, "cells", 1)
    a_own, own_h, own_l = corner_of(own3, modes, scale)
    oth3, a_own, own_h, own_l = together((oth3, a_own, own_h, own_l))
    given = (own_h, own_l, a_own, a0, a1, *sums)
    return tuple(main(scal, own3, oth3, tables, ridge_panel, given, rows, cols, scale))


def solution(mesh):
    return jax.shard_map(
        per_device,
        mesh=mesh,
        in_specs=(P("snap", "cells"), P(None, "cells"), P("cells"), P()),
        out_specs=(P("cells", "snap"), P("cells", None)),
        check_vma=False,
    )
```

```python
import functools
import math

import jax
import jax.numpy as jnp
import numpy as np
from jax import lax
from jax.experimental import pallas as pl
from jax.experimental.pallas import tpu as pltpu
from jax.sharding import PartitionSpec as P

PANEL = 512
HI = lax.Precision.HIGHEST
HALF = 256
BLOCK = 128
STEP = 32
SLOTS = 112
F32 = jnp.float32
BF16 = jnp.bfloat16
NT = (((1,), (1,)), ((), ()))
TN = (((0,), (0,)), ((), ()))
NN = (((1,), (0,)), ((), ()))


def dot(a, b, dims, precision=None):
    return lax.dot_general(a, b, dims, precision=precision, preferred_element_type=F32)


def split(value):
    high = value.astype(BF16)
    return high, (value - high.astype(F32)).astype(BF16)


def dot3(a, b):
    ah, al = a
    bh, bl = b
    return dot(jnp.concatenate([ah, ah, al], 1), jnp.concatenate([bh, bl, bh], 1), NT)


def pick_tables(first, rows, modes):
    index = first + lax.broadcasted_iota(jnp.int32, (rows, 128), 0)
    slot = lax.broadcasted_iota(jnp.int32, (rows, 128), 1)

    def offset(a):
        return modes + modes * a - (a * (a - 1)) // 2

    linear = index < modes
    here = (index >= offset(slot)) & (index < offset(slot + 1)) & (slot < modes)
    right_value = jnp.where(here, index - offset(slot) + slot, 0).astype(F32)
    right_index = jnp.sum(right_value, axis=1, keepdims=True).astype(jnp.int32)
    left_index = jnp.sum(jnp.where(here, slot, 0).astype(F32), axis=1, keepdims=True).astype(jnp.int32)
    left_index = jnp.where(linear, index, left_index)
    right_index = jnp.where(linear, modes, right_index)
    return (slot == left_index).astype(F32), (slot == right_index).astype(F32)


def pick_kernel(modes, scale, scal, lr, rr, lc, rc):
    for ref_l, ref_r, first in ((lr, rr, scal[0]), (lc, rc, scal[1])):
        block = math.gcd(lr.shape[0], ref_l.shape[0])

        def rows_body(i, carry, ref_l=ref_l, ref_r=ref_r, first=first):
            at = pl.ds(pl.multiple_of(i * block, 16), block)
            left, right = pick_tables(first + i * block, block, modes)
            for ref, value in ((ref_l, left * scale), (ref_r, right)):
                ref[at, 0:SLOTS] = value[:, 0:SLOTS].astype(BF16)
                ref[at, SLOTS : 2 * SLOTS] = value[:, 0:SLOTS].astype(BF16)
            return carry

        lax.fori_loop(0, ref_l.shape[0] // block, rows_body, 0)


def picks(scal, row_pad, col_pad, modes, scale):
    shapes = [(row_pad, 2 * SLOTS)] * 2 + [(col_pad, 2 * SLOTS)] * 2
    return pl.pallas_call(
        functools.partial(pick_kernel, modes, scale),
        in_specs=[pl.BlockSpec(memory_space=pltpu.SMEM)],
        out_shape=[jax.ShapeDtypeStruct(s, BF16) for s in shapes],
        compiler_params=pltpu.CompilerParams(vmem_limit_bytes=40 * 2**20),
        name="picks",
    )(scal)


def panel_features(c_ref, t, f_ref, modes, scale):
    f_ref[0:modes, :] = c_ref[t] * scale
    at, a = modes, 0
    while at < PANEL:
        count = min(modes - a, PANEL - at)
        f_ref[at : at + count, :] = c_ref[t, a : a + count, :] * (c_ref[t, a : a + 1, :] * scale)
        at += count
        a += 1


def panel_one(t, c_s, f_ref, fh, fl, modes, scale):
    panel_features(c_s, t, f_ref, modes, scale)
    fh[t], fl[t] = split(f_ref[...])


def panel_pair(t, c_s, f_s, fh, fl, modes, scale):
    for i in range(2):
        panel_one(t + i, c_s, f_s.at[i], fh, fl, modes, scale)


def corner_one(t, fh, fl, at):
    h, l = fh[t], fl[t]
    rows = slice(at, at + HALF)
    return dot3((h[rows], l[rows]), (h[at:], l[at:]))


def corner_part(t, fh, fl, at):
    return corner_one(t, fh, fl, at) + corner_one(t + 1, fh, fl, at)


def corner_pair(t, fh, fl, a_ref):
    a_ref[0:HALF, :] = corner_part(t, fh, fl, 0)
    a_ref[HALF:, HALF:] = corner_part(t, fh, fl, HALF)


def lane_bcast(x, c):
    return jnp.broadcast_to(x[:, c : c + 1], (8, 128))


def sub_bcast(x, k):
    return jnp.broadcast_to(x[k : k + 1, :], (8, 128))


def split3(value):
    high = value.astype(BF16)
    rest = value - high.astype(F32)
    middle = rest.astype(BF16)
    return high, middle, (rest - middle.astype(F32)).astype(BF16)


def update_dot(left, right):
    lh, lm, ll = split3(left)
    rh, rm, rl = split3(right)
    return dot(
        jnp.concatenate([lh, lh, lh, lm, lm, ll], 0), jnp.concatenate([rh, rm, rl, rh, rm, rh], 0), TN
    )


def factor_step(s_ref, b, between):
    lo = STEP * b
    strips = STEP // 8
    sub = lax.broadcasted_iota(jnp.int32, (8, 128), 0)
    T = [[s_ref[lo + 8 * r : lo + 8 * r + 8, 0:128], s_ref[lo + 8 * r : lo + 8 * r + 8, 128:256]] for r in range(strips)]
    for q in range(strips):
        cols = range(8 * q, 8 * q + 8)
        B = {(r, j): lane_bcast(T[r][0], lo + j) for j in cols for r in range(q, strips)}
        scale = None
        for k in cols:
            rs = lax.rsqrt(sub_bcast(B[q, k], k - 8 * q))
            inv = rs * rs
            scale = rs if scale is None else jnp.where(sub == k - 8 * q, rs, scale)
            row = [sub_bcast(part, k - 8 * q) for part in T[q]]
            pivots = {j: sub_bcast(B[q, k], j - 8 * q) for j in range(k + 1, 8 * q + 8)}
            for r in range(q, strips):
                m = B[r, k] * inv
                if r == q:
                    m = jnp.where(sub > k - 8 * q, m, 0.0)
                for j in pivots:
                    B[r, j] = B[r, j] - m * pivots[j]
                T[r] = [part - m * line for part, line in zip(T[r], row)]
        T[q] = [part * scale for part in T[q]]
        between(4 * b + q)
    for r in range(strips):
        s_ref[lo + 8 * r : lo + 8 * r + 8, 0:128] = T[r][0]
        s_ref[lo + 8 * r : lo + 8 * r + 8, 128:256] = T[r][1]
    if b < 3:
        full = s_ref[lo : lo + STEP, :]
        upd = update_dot(full[:, 0:128], full)
        s_ref[lo + STEP : 128, :] -= upd[lo + STEP :, :]


def factor_block(k, a_s, s_ref, e_s, u_s, inv_s, low_s, between):
    lo, hi = BLOCK * k, BLOCK * (k + 1)
    ri = lax.broadcasted_iota(jnp.int32, (BLOCK, BLOCK), 0)
    ci = lax.broadcasted_iota(jnp.int32, (BLOCK, BLOCK), 1)
    s_ref[:, 0:BLOCK] = a_s[lo:hi, lo:hi]
    s_ref[:, BLOCK:] = (ri == ci).astype(F32)
    for b in range(4):
        factor_step(s_ref, b, between)
    inverse = s_ref[:, BLOCK:]
    inv_s[k] = inverse
    if hi < PANEL:
        rest = dot(inverse, a_s[lo:hi, hi:], NN, HI)
        u_s[lo:hi, hi:] = rest
        a_s[hi : hi + BLOCK, hi:] -= dot(rest[:, 0:BLOCK], rest, TN, HI)
        if hi + BLOCK < PANEL:
            far = rest[:, BLOCK:]
            a_s[hi + BLOCK :, hi + BLOCK :] -= dot(far, far, TN, HI)
    if k % 2:
        low_s[k // 2] = dot(inverse, e_s[...], NN, HI)
    else:
        e_s[...] = -dot(rest[:, 0:BLOCK], inverse, TN, HI)


def stacked(c, modes):
    n = c.shape[1]
    high, low = split(c)
    gap = lax.broadcasted_iota(jnp.int32, (SLOTS - modes, n), 0)
    ones = (gap == 0).astype(F32).astype(BF16)
    none = jnp.zeros((SLOTS - modes, n), BF16)
    return jnp.concatenate([high, ones, low, none], axis=0)


def picked(left, right, cs):
    return split(dot(left, cs, NN) * dot(right, cs, NN))


def block_parts(t, c_s, fh, fl, lr, rr, lc, rc, gr, gc, gt, modes, start=None):
    env = {}
    gr_was, gc_was, gt_was = start or (gr, gc, gt)

    def part0():
        cs = stacked(c_s[t], modes)
        env["fr"] = picked(lr[...], rr[...], cs)
        env["fc"] = picked(lc[...], rc[...], cs)
        env["fp"] = (fh[t], fl[t])

    def part1():
        value = dot3(env["fr"], env["fp"])
        gr[...] = value if gr_was is None else gr_was[...] + value

    def part2(at):
        gc[at, :] = gc_was[at, :] + dot3(tuple(half[at] for half in env["fc"]), env["fp"])

    def part3():
        gt[...] = gt_was[...] + dot3(env["fr"], env["fc"])

    mid = gc.shape[0] // 2
    lower, upper = slice(0, mid), slice(mid, 2 * mid)
    return [part0, part1, lambda: part2(lower), part3, lambda: part2(upper)]


def pair_inverse(p, inv_s, low_s):
    zero = jnp.zeros((BLOCK, BLOCK), F32)
    top = jnp.concatenate([inv_s[2 * p], zero], 1)
    return jnp.concatenate([top, jnp.concatenate([low_s[p], inv_s[2 * p + 1]], 1)], 0)


def diagonal(shape, first_row, first_col, values):
    ri = first_row + lax.broadcasted_iota(jnp.int32, shape, 0)
    ci = first_col + lax.broadcasted_iota(jnp.int32, shape, 1)
    return jnp.where(ri == ci, values, 0.0)


def diagonal(shape, first_row, first_col, values):
    ri = first_row + lax.broadcasted_iota(jnp.int32, shape, 0)
    ci = first_col + lax.broadcasted_iota(jnp.int32, shape, 1)
    return jnp.where(ri == ci, values, 0.0)


def start_kernel(modes, scale, own, lr, rr, lc, rc, scal, ridge_panel, ridge_cols, a_out, gr, gc, gt, f_s, fh, fl):
    gc[...] = diagonal(gc.shape, scal[1], 0, ridge_panel[...])
    gt[...] = diagonal(gt.shape, scal[0], scal[1], ridge_cols[...])
    panel_one(0, own, f_s, fh, fl, modes, scale)
    a_out[0:HALF, :] = corner_one(0, fh, fl, 0)
    a_out[HALF:, HALF:] = corner_one(0, fh, fl, HALF)
    for part in block_parts(0, own, fh, fl, lr, rr, lc, rc, gr, gc, gt, modes, (None, gc, gt)):
        part()


def early_kernel(modes, scale, first, *refs):
    own, oth, lr, rr, lc, rc = refs[0:6]
    if first:
        a_in, gr_in, gc_in, gt_in = refs[6:10]
        a_out, gr, gr_oth, gc, gt, c_s, f_s, fh, fl, a_s, pair_s = refs[10:]
    else:
        gr_in, gr_oth_in, gc_in, gt_in = refs[6:10]
        a_out, gr, gr_oth, gc, gt, c_s, f_s, fh, fl, a_s, pair_s = refs[10:]
    for i in range(2):
        c_s[i] = own[i]
        c_s[2 + i] = oth[i]

    def add(t, rows, start):
        for part in block_parts(t, c_s, fh, fl, lr, rr, lc, rc, rows, gc, gt, modes, start):
            part()

    if first:
        panel_one(1, c_s, f_s.at[0], fh, fl, modes, scale)
        panel_pair(2, c_s, f_s, fh, fl, modes, scale)
        corner_pair(2, fh, fl, a_out)
        a_out[0:HALF, :] += a_in[0:HALF, :] + corner_one(1, fh, fl, 0)
        a_out[HALF:, HALF:] += a_in[HALF:, HALF:] + corner_one(1, fh, fl, HALF)
        add(1, gr, (gr_in, gc_in, gt_in))
        add(2, gr_oth, (None, gc, gt))
        add(3, gr_oth, None)
        return
    for i in range(2):
        panel_pair(2 * i, c_s, f_s, fh, fl, modes, scale)
        corner_pair(2 * i, fh, fl, a_s.at[i])
    a_out[...] = a_s[0] + a_s[1]
    gc[...] = gc_in[...]
    gt[...] = gt_in[...]

    def pair_body(i, carry):
        add(2 * i, pair_s.at[i], (None, gc, gt))
        add(2 * i + 1, pair_s.at[i], None)
        return carry

    lax.fori_loop(0, 2, pair_body, 0)
    gr[...] = gr_in[...] + pair_s[0]
    gr_oth[...] = gr_oth_in[...] + pair_s[1]


def start(own, tables, scal, ridge_panel, ridge_cols, modes, scale):
    lr, rr, lc, rc = tables
    row_pad, col_pad = lr.shape[0], lc.shape[0]
    n = own.shape[2]
    vmem = pl.BlockSpec(memory_space=pltpu.VMEM)
    shapes = [(PANEL, PANEL), (row_pad, PANEL), (col_pad, PANEL), (row_pad, col_pad)]
    return pl.pallas_call(
        functools.partial(start_kernel, modes, scale),
        in_specs=[vmem] * 5 + [pl.BlockSpec(memory_space=pltpu.SMEM)] + [vmem] * 2,
        out_specs=[vmem] * 4,
        out_shape=[jax.ShapeDtypeStruct(s, F32) for s in shapes],
        scratch_shapes=[
            pltpu.VMEM((PANEL, n), F32),
            pltpu.VMEM((1, PANEL, n), BF16),
            pltpu.VMEM((1, PANEL, n), BF16),
        ],
        compiler_params=pltpu.CompilerParams(vmem_limit_bytes=24 * 2**20),
        cost_estimate=pl.CostEstimate(flops=10**9, bytes_accessed=2**22, transcendentals=0),
        name="early_start",
    )(own, lr, rr, lc, rc, scal, ridge_panel, ridge_cols)


def early(own, oth, tables, rest, first, modes, scale, cost):
    lr, rr, lc, rc = tables
    row_pad, col_pad = lr.shape[0], lc.shape[0]
    n = own.shape[2]
    vmem = pl.BlockSpec(memory_space=pltpu.VMEM)
    held = 4
    shapes = [(PANEL, PANEL)] + [(row_pad, PANEL)] * 2 + [(col_pad, PANEL), (row_pad, col_pad)]
    return pl.pallas_call(
        functools.partial(early_kernel, modes, scale, first),
        in_specs=[vmem] * (6 + len(rest)),
        out_specs=[vmem] * len(shapes),
        out_shape=[jax.ShapeDtypeStruct(s, F32) for s in shapes],
        scratch_shapes=[
            pltpu.VMEM((held, modes, n), F32),
            pltpu.VMEM((2, PANEL, n), F32),
            pltpu.VMEM((held, PANEL, n), BF16),
            pltpu.VMEM((held, PANEL, n), BF16),
            pltpu.VMEM((2, PANEL, PANEL), F32),
            pltpu.VMEM((2, row_pad, PANEL), F32),
        ],
        compiler_params=pltpu.CompilerParams(vmem_limit_bytes=32 * 2**20),
        cost_estimate=pl.CostEstimate(flops=cost, bytes_accessed=2**22, transcendentals=0),
        name="early_first" if first else "early_second",
    )(own, oth, lr, rr, lc, rc, *rest)


def corner_kernel(modes, scale, c_ref, a_out, fh, fl, f_s):
    for i in range(2):
        panel_pair(2 * i, c_ref, f_s, fh, fl, modes, scale)
        corner_pair(2 * i, fh, fl, a_out.at[i])


def corner_of(own, modes, scale):
    n = own.shape[2]
    vmem = pl.BlockSpec(memory_space=pltpu.VMEM)
    return pl.pallas_call(
        functools.partial(corner_kernel, modes, scale),
        in_specs=[vmem],
        out_specs=[vmem] * 3,
        out_shape=[
            jax.ShapeDtypeStruct((2, PANEL, PANEL), F32),
            jax.ShapeDtypeStruct((4, PANEL, n), BF16),
            jax.ShapeDtypeStruct((4, PANEL, n), BF16),
        ],
        scratch_shapes=[pltpu.VMEM((2, PANEL, n), F32)],
        compiler_params=pltpu.CompilerParams(vmem_limit_bytes=24 * 2**20),
        cost_estimate=pl.CostEstimate(flops=10**9, bytes_accessed=2**22, transcendentals=0),
        name="late_corner",
    )(own)


def halves_kernel(core_ref, part, offset, keep, send):
    core = core_ref[0]
    half = keep.shape[1]
    mine = pl.multiple_of(core * half, half)
    other = pl.multiple_of((1 - core) * half, half)
    send[...] = (part[pl.ds(other, half), :] - offset[...]).T
    keep[...] = (part[pl.ds(mine, half), :] - offset[...]).T


def halves(core, part, offset):
    vmem = pl.BlockSpec(memory_space=pltpu.VMEM)
    snaps, modes = part.shape
    return pl.pallas_call(
        halves_kernel,
        in_specs=[pl.BlockSpec(memory_space=pltpu.SMEM)] + [vmem] * 2,
        out_specs=[vmem] * 2,
        out_shape=[jax.ShapeDtypeStruct((modes, snaps // 2), F32)] * 2,
        compiler_params=pltpu.CompilerParams(vmem_limit_bytes=16 * 2**20),
        name="halves",
    )(core, part, offset)


LATE = 8


def main_kernel(modes, scale, scal, own, oth, lr, rr, lc, rc, ridge_panel,
                own_h, own_l, a_own, a0, a1, gr_in, gr_oth_in, gc_in, gt_in,
                tile_out, rows_out,
                f_s, fh, fl, a_p, a_s, s_s, e_s, u_s, inv_s, low_s, gr, gc, gt, pr, pc):
    first_row, first_col = scal[0], scal[1]
    rows, cols = tile_out.shape

    def corner_body(i, carry):
        panel_pair(2 * i, oth, f_s, fh, fl, modes, scale)
        a_p[i] = corner_part(2 * i, fh, fl, 0)
        return carry

    lax.fori_loop(0, 2, corner_body, 0)
    a_s[...] = diagonal(a_s.shape, 0, 0, ridge_panel[...])

    def add_corner(rows, cols, late):
        early_sum = a0[rows, cols] + a1[rows, cols]
        a_s[rows, cols] += early_sum + ((a_own[0, rows, cols] + late[0]) + (a_own[1, rows, cols] + late[1]))

    def add_low():
        half = slice(HALF, PANEL)
        add_corner(half, half, [corner_part(2 * i, fh, fl, HALF) for i in range(2)])

    add_corner(slice(0, HALF), slice(0, PANEL), a_p)

    parts = []
    for t in range(LATE):
        held = (own, own_h, own_l) if t < 4 else (oth, fh, fl)
        pair = gr.at[t // 2]
        start = (pair if t % 2 else None, gc if t else gc_in, gt if t else gt_in)
        parts += block_parts(t % 4, *held, lr, rr, lc, rc, pair, gc, gt, modes, start)

    def solve_first(p, at, g):
        first = dot(g[:, 0:HALF], pair_inverse(0, inv_s, low_s), NT, HI)
        p[at, 0:HALF] = first
        p[at, HALF:] = g[:, HALF:] - dot(first, u_s[0:HALF, HALF:], NN, HI)

    def solve_rows():
        line = diagonal(pr.shape, first_row, 0, ridge_panel[...])
        sums = (gr_in[...] + (gr[0] + gr[1])) + (gr_oth_in[...] + (gr[2] + gr[3])) + line
        solve_first(pr, slice(0, pr.shape[0]), sums)

    def solve_cols(i):
        mid = pc.shape[0] // 2
        at = slice(mid * i, mid * i + mid)
        solve_first(pc, at, gc[at, :])

    def update(at):
        ri = first_row + lax.broadcasted_iota(jnp.int32, gt.shape, 0)
        ci = first_col + lax.broadcasted_iota(jnp.int32, gt.shape, 1)
        change = dot3(split(pr[:, at : at + HALF]), split(pc[:, at : at + HALF]))
        return gt[...] - jnp.where((ri >= PANEL) & (ci >= PANEL), change, 0.0)

    def write_rows(at):
        line = first_row + lax.broadcasted_iota(jnp.int32, (rows, HALF), 0)
        place = at + lax.broadcasted_iota(jnp.int32, (rows, HALF), 1)
        rows_out[:, at : at + HALF] = jnp.where(place <= line, pr[0:rows, at : at + HALF], 0.0)

    def update_first():
        gt[...] = update(0)
        write_rows(0)

    slots = [[] for _ in range(64)]
    for i, part in enumerate(parts):
        slots[i * 50 // len(parts)].append(part)
    slots[20].append(add_low)
    slots[51].append(solve_rows)
    slots[53].append(lambda: solve_cols(0))
    slots[55].append(lambda: solve_cols(1))
    slots[58].append(update_first)

    def between_of(k):
        def between(i):
            for part in slots[16 * k + i]:
                part()

        return between

    for k in range(4):
        factor_block(k, a_s, s_s, e_s, u_s, inv_s, low_s, between_of(k))

    inverse = pair_inverse(1, inv_s, low_s)
    for p in (pr, pc):
        p[:, HALF:] = dot(p[:, HALF:], inverse, NT, HI)
    tile_out[...] = update(HALF)[0:rows, 0:cols]
    write_rows(HALF)


def main(scal, own, oth, tables, ridge_panel, sums, rows, cols, scale):
    modes, n = own.shape[1:]
    lr, rr, lc, rc = tables
    row_pad, col_pad = lr.shape[0], lc.shape[0]
    vmem = pl.BlockSpec(memory_space=pltpu.VMEM)
    return pl.pallas_call(
        functools.partial(main_kernel, modes, scale),
        in_specs=[pl.BlockSpec(memory_space=pltpu.SMEM)] + [vmem] * 16,
        out_specs=[vmem, vmem],
        out_shape=[jax.ShapeDtypeStruct((rows, cols), F32), jax.ShapeDtypeStruct((rows, PANEL), F32)],
        scratch_shapes=[
            pltpu.VMEM((2, PANEL, n), F32),
            pltpu.VMEM((4, PANEL, n), BF16),
            pltpu.VMEM((4, PANEL, n), BF16),
            pltpu.VMEM((2, HALF, PANEL), F32),
            pltpu.VMEM((PANEL, PANEL), F32),
            pltpu.VMEM((BLOCK, 2 * BLOCK), F32),
            pltpu.VMEM((BLOCK, BLOCK), F32),
            pltpu.VMEM((PANEL, PANEL), F32),
            pltpu.VMEM((4, BLOCK, BLOCK), F32),
            pltpu.VMEM((2, BLOCK, BLOCK), F32),
            pltpu.VMEM((LATE // 2, row_pad, PANEL), F32),
            pltpu.VMEM((col_pad, PANEL), F32),
            pltpu.VMEM((row_pad, col_pad), F32),
            pltpu.VMEM((row_pad, PANEL), F32),
            pltpu.VMEM((col_pad, PANEL), F32),
        ],
        compiler_params=pltpu.CompilerParams(vmem_limit_bytes=32 * 2**20),
        name="gram_factor",
    )(scal, own, oth, lr, rr, lc, rc, ridge_panel, *sums)


def swap(value, axis, bit, other_bit=None):
    size = lax.axis_size(axis)
    bits = (bit, bit if other_bit is None else other_bit)
    return lax.ppermute(value, axis, [(i, i ^ bits[i & 1]) for i in range(size)])


def padded(count):
    return -(-count // 16) * 16


def per_device(snapshots, pod_basis, reference_field, ridge_weights):
    modes = pod_basis.shape[0]
    snap_total = snapshots.shape[0] * lax.axis_size("snap")
    scale = snap_total**-0.5
    feature_total = ridge_weights.shape[0]
    rows = feature_total // lax.axis_size("cells")
    cols = feature_total // lax.axis_size("snap")
    group = lax.axis_index("snap")
    core = lax.axis_index("cells") & 1
    first_row = lax.axis_index("cells") * rows
    first_col = group * cols
    scal = jnp.stack([first_row, first_col]).astype(jnp.int32)
    tables = picks(scal, padded(rows), padded(cols), modes, scale)
    ridge_panel = ridge_weights[None, :PANEL]
    ridge_cols = lax.dynamic_slice_in_dim(ridge_weights, first_col, cols)
    ridge_cols = jnp.pad(ridge_cols, (0, padded(cols) - cols))[None, :]

    projected = lax.dot_general(snapshots, pod_basis, NT, preferred_element_type=F32)
    offset = lax.dot_general(reference_field[None, :], pod_basis, NT, preferred_element_type=F32)
    keep, send = halves(core[None].astype(jnp.int32), projected, offset)
    total = keep + swap(send, "cells", 1)
    together = lax.optimization_barrier
    for bit, other_bit in ((2, 4), (4, 2), (8, 8)):
        got = swap(total, "cells", bit, other_bit)
        if bit == 4:
            got, tables, ridge_panel, ridge_cols = together((got, tables, ridge_panel, ridge_cols))
        total = total + got

    own0 = total[None]
    own1 = swap(own0, "snap", 4)
    oth0 = swap(own0, "cells", 1)
    sums = start(own0, tables, scal, ridge_panel, ridge_cols, modes, scale)
    own1, oth0, *sums = together((own1, oth0, *sums))
    pair = jnp.concatenate([own0, own1], 0)
    own2 = swap(pair, "snap", 2)
    oth_pair = jnp.concatenate([oth0, swap(own1, "cells", 1)], 0)
    sums = early(pair, oth_pair, tables, sums, True, modes, scale, 4 * 10**9)
    near = swap(pair, "snap", 1)
    own2, near, a0, *sums = together((own2, near, *sums))
    far = swap(own2, "snap", 1)
    oth2 = swap(own2, "cells", 1)
    sums = early(own2, oth2, tables, sums, False, modes, scale, 4 * 10**9)
    far, a1, *sums = together((far, *sums))
    own3 = jnp.concatenate([near, far], 0)
    oth3 = swap(own3, "cells", 1)
    a_own, own_h, own_l = corner_of(own3, modes, scale)
    oth3, a_own, own_h, own_l = together((oth3, a_own, own_h, own_l))
    given = (own_h, own_l, a_own, a0, a1, *sums)
    return tuple(main(scal, own3, oth3, tables, ridge_panel, given, rows, cols, scale))


def solution(mesh):
    return jax.shard_map(
        per_device,
        mesh=mesh,
        in_specs=(P("snap", "cells"), P(None, "cells"), P("cells"), P()),
        out_specs=(P("cells", "snap"), P("cells", None)),
        check_vma=False,
    )
```
